512 devices in a mesh: segment: 4 (over z_hi), seq: 32 (over y, x), dp: 4 (over z_lo, core).
Axes of the slice: x: 4, y: 8, z: 8 (z_hi: 4, z_lo: 2; z = z_hi * 2 + z_lo), core: 2. Of those that a mesh axis runs over, the one named last changes fastest.
Arguments:
- decoder_queries: bfloat16 [4, 4, 2048, 4096], P('segment', 'dp', None, 'seq'), may hold values from -95 to 95
- decoder_keys: bfloat16 [4, 4, 2048, 4096], P('segment', 'dp', None, 'seq'), may hold values from -2.1 to 2.1
- decoder_values: bfloat16 [4, 4, 2048, 4096], P('segment', 'dp', None, 'seq'), may hold values from -6 to 6
- cross_queries: bfloat16 [4, 4, 2048, 4096], P('segment', 'dp', None, 'seq'), may hold values from -95 to 95
- memory_keys: bfloat16 [4, 4, 2048, 512], P('segment', 'dp', None, 'seq'), may hold values from -2.1 to 2.1
- memory_values: bfloat16 [4, 4, 2048, 512], P('segment', 'dp', None, 'seq'), may hold values from -6 to 6
- target_lengths: int32 [4, 4, 2], P('segment', 'dp'), may hold values from 512 to 2048, as said below
- source_lengths: int32 [4, 4, 2], P('segment', 'dp'), may hold values from 64 to 256, as said below
Outputs:
- mixed: bfloat16 [4, 4, 2048, 4096], P('segment', 'dp', None, 'seq')
The draws below stay inside these ranges and needn't reach their ends.
Inputs may be any that keep to these rules, and one draw needn't show every extreme that they name: `target_lengths`: some sequence has exactly 2048 live tokens and some other exactly 512. `source_lengths`: some sequence has exactly 256 live memory tokens and some other exactly 64.
All inputs are finite; a program needn't handle non-finite values.
Results may differ from the reference program's by a relative error of at most 0.0057.
Values may be sent and summed in bfloat16 or wider, within the bound.
A program may use at most 64 MiB of HBM per device.

```python
import jax
import jax.numpy as jnp
from jax import lax

HEADS = 32
HS = 64
SEQS = 2
HD = 2048
L = 2048
M = 256
N_SEGMENT = 4
N_DP = 4


def decoder_base(key):
    return jnp.clip(0.35 * jax.random.normal(jax.random.fold_in(key, 101), (N_SEGMENT, N_DP, HD, SEQS * L), jnp.float32), -2.1, 2.1)


def memory_base(key):
    return jnp.clip(0.35 * jax.random.normal(jax.random.fold_in(key, 202), (N_SEGMENT, N_DP, HD, SEQS * M), jnp.float32), -2.1, 2.1)


def draw_decoder_keys(key, part):
    return decoder_base(key).astype(jnp.bfloat16)


def draw_memory_keys(key, part):
    return memory_base(key).astype(jnp.bfloat16)


def draw_decoder_queries(key, part):
    key = jax.random.fold_in(key, 3)
    shape = (N_SEGMENT, N_DP, HD, SEQS * L)
    result = jnp.clip(0.35 * jax.random.normal(key, shape, jnp.float32), -2.1, 2.1)
    return result.astype(jnp.bfloat16)


def draw_cross_queries(key, part):
    key = jax.random.fold_in(key, 4)
    shape = (N_SEGMENT, N_DP, HD, SEQS * L)
    result = jnp.clip(0.35 * jax.random.normal(key, shape, jnp.float32), -2.1, 2.1)
    return result.astype(jnp.bfloat16)


def length_table(key, longest):
    count = N_SEGMENT * N_DP * SEQS
    values = jax.random.randint(key, (count,), longest // 4, longest + 1)
    chosen = jax.random.randint(jax.random.fold_in(key, 1), (), 0, count)
    second = (chosen + 1 + jax.random.randint(jax.random.fold_in(key, 2), (), 0, count - 1)) % count
    places = jnp.arange(count)
    values = jnp.where(places == chosen, longest, jnp.where(places == second, longest // 4, values))
    return values.reshape(N_SEGMENT, N_DP, SEQS).astype(jnp.int32)


def draw_target_lengths(key, part):
    key = jax.random.fold_in(key, 5)
    return length_table(key, L)


def draw_source_lengths(key, part):
    key = jax.random.fold_in(key, 6)
    return length_table(key, M)


def levels(rng, extent, shards, least, largest):
    factor_of, own = 1.0, jax.random.fold_in(rng, 6)
    for dim, shards_of in shards:
        heights = jnp.exp(jax.random.uniform(jax.random.fold_in(own, dim), (shards_of,), jnp.float32, least / len(shards), largest / len(shards)))
        factor_of = factor_of * jnp.repeat(heights, extent[dim] // shards_of).reshape([-1 if axis == dim else 1 for axis in range(len(extent))])
    return factor_of


def noise(stream_key, dims, scale, most, shards=(), kind=jnp.bfloat16):
    drawn = scale * jax.random.normal(stream_key, dims, jnp.float32)
    if shards:
        drawn = drawn * levels(stream_key, dims, shards, -0.22, 0.18)
    return jnp.clip(drawn, -most, most).astype(kind)


def setup_inputs(seed: int = 0) -> dict:
    arg_keys = jax.random.split(jax.random.key(seed), 9)
    return {
        "decoder_queries": draw_decoder_queries(jax.random.fold_in(arg_keys[8], 71), 0),
        "decoder_keys": draw_decoder_keys(jax.random.fold_in(arg_keys[8], 71), 0),
        "decoder_values": noise(arg_keys[2], (N_SEGMENT, N_DP, HD, SEQS * L), 1.0, 6.0, ((0, 4), (1, 4), (3, 32))),
        "cross_queries": draw_cross_queries(jax.random.fold_in(arg_keys[8], 71), 0),
        "memory_keys": draw_memory_keys(jax.random.fold_in(arg_keys[8], 71), 0),
        "memory_values": noise(arg_keys[5], (N_SEGMENT, N_DP, HD, SEQS * M), 1.0, 6.0, ((0, 4), (1, 4), (3, 32))),
        "target_lengths": draw_target_lengths(jax.random.fold_in(arg_keys[8], 71), 0),
        "source_lengths": draw_source_lengths(jax.random.fold_in(arg_keys[8], 71), 0),
    }


def attend(queried, key_rows, value_rows, allowed):
    scores = jnp.dot(queried.astype(jnp.float32).T, key_rows.astype(jnp.float32), precision=lax.Precision.HIGHEST)
    scores = jnp.where(allowed, scores, -1e30)
    highest = jnp.max(scores, axis=1, keepdims=True)
    weights = jnp.exp(scores - highest)
    summed = jnp.sum(weights, axis=1, keepdims=True)
    chances = (weights / summed).astype(jnp.bfloat16)
    context = jnp.dot(value_rows.astype(jnp.float32), chances.astype(jnp.float32).T, precision=lax.Precision.HIGHEST)
    return context.astype(jnp.bfloat16)


def reference(decoder_queries, decoder_keys, decoder_values, cross_queries, memory_keys, memory_values, target_lengths, source_lengths):
    micro = N_SEGMENT * N_DP
    relayed_keys = jnp.roll(memory_keys, 1, axis=0)
    relayed_values = jnp.roll(memory_values, 1, axis=0)

    def heads(array, width):
        shaped = array.reshape(micro, HEADS, HS, SEQS, width)
        shaped = jnp.transpose(shaped, (0, 3, 1, 2, 4))
        return shaped.reshape(micro * SEQS * HEADS, HS, width)

    target_each = jnp.repeat(target_lengths.reshape(micro * SEQS), HEADS)
    source_each = jnp.repeat(source_lengths.reshape(micro * SEQS), HEADS)
    positions = jnp.arange(L)[:, None]
    columns = jnp.arange(L)[None, :]
    memory_columns = jnp.arange(M)[None, :]

    def one_head(members):
        queried, key_rows, value_rows, crossed, mem_keys, mem_values, target_limit, source_limit = members
        allowed = (columns <= positions) & (columns < target_limit)
        self_part = attend(queried, key_rows, value_rows, allowed)
        cross_part = attend(crossed, mem_keys, mem_values, memory_columns < source_limit)
        return self_part, cross_part

    self_all, cross_all = lax.map(one_head, (heads(decoder_queries, L), heads(decoder_keys, L), heads(decoder_values, L), heads(cross_queries, L), heads(relayed_keys, M), heads(relayed_values, M), target_each, source_each))

    def back(array):
        shaped = array.reshape(micro, SEQS, HEADS, HS, L)
        shaped = jnp.transpose(shaped, (0, 2, 3, 1, 4))
        return shaped.reshape(N_SEGMENT, N_DP, HD, SEQS * L)

    self_context = back(self_all)
    cross_context = back(cross_all)
    live_count = jnp.sum(target_lengths).astype(jnp.float32)
    scale = jnp.float32(micro * SEQS * L) / live_count
    places = jnp.arange(SEQS * L)
    within = places % L
    which = places // L
    limits = target_lengths[:, :, which]
    weight = jnp.where(within[None, None, :] < limits, scale, jnp.float32(0.0))
    mixed = (self_context.astype(jnp.float32) + cross_context.astype(jnp.float32)) * weight[:, :, None, :]
    return mixed.astype(jnp.bfloat16)
```

```python
import functools

import jax
import jax.numpy as jnp
from jax import lax
from jax.experimental import pallas as pl
from jax.experimental.pallas import tpu as pltpu
from jax.sharding import PartitionSpec as P

HS = 64
SEQS = 2
BLOCK = 256
MASKED = -1e30
MESH = pl.DeviceIdType.MESH


def kernel(
    n_seg, n_seq, n_dp,
    target_ref, source_ref, dq_ref, dk_ref, dv_ref, cq_ref, mk_ref, mv_ref,
    out_ref,
    q_buf, k_buf, v_buf, c_buf, mk_buf, mv_buf, kt_buf, mvt_buf, o_buf, len_own, len_all,
    in_sems, mem_sem, len_sem, out_sem, send_sem, mem_send, len_send, out_send,
):
    group = n_seq // SEQS
    tokens = dq_ref.shape[1]
    seq_len = group * tokens
    mem_tokens = mk_ref.shape[0]
    heads = q_buf.shape[0]
    owned = heads * HS
    replicas = n_seg * n_dp

    seg, place, dp = lax.axis_index("segment"), lax.axis_index("seq"), lax.axis_index("dp")
    which = place // group
    rank = place % group
    first = which * group
    own = seg * n_dp + dp
    target = target_ref[0, 0, which]
    source = source_ref[0, 0, which]

    def partner(step):
        return (rank + step) % group

    def other(step):
        index = (own + step) % replicas
        return {"segment": index // n_dp, "dp": index % n_dp}

    later_seg = (seg + 1) % n_seg
    early_seg = (seg + n_seg - 1) % n_seg

    row = lax.broadcasted_iota(jnp.int32, (HS, seq_len), 0)
    column = lax.broadcasted_iota(jnp.int32, (HS, seq_len), 1)
    one_row = jnp.where(row == 0, 1.0, 0.0).astype(jnp.bfloat16)
    mask_row = jnp.where((row == 0) & (column >= target), MASKED, 0.0).astype(jnp.bfloat16)
    for h in range(heads):
        q_buf[h, HS:, :] = one_row
        k_buf[h, HS:, :] = mask_row
        v_buf[h, HS:, :] = one_row[:16]
        c_buf[h, (1 - h) * HS : (2 - h) * HS, :] = one_row
    lens = jnp.full(len_own.shape, target_ref[0, 0, 0] + target_ref[0, 0, 1], jnp.int32)
    len_own[...] = lens
    len_all[own] = lens

    barrier = pltpu.get_barrier_semaphore()

    @pl.loop(1, group)
    def _(step):
        pl.semaphore_signal(barrier, 1, device_id={"seq": first + partner(step)}, device_id_type=MESH)

    @pl.loop(0, group)
    def _(step):
        pl.semaphore_signal(
            barrier, 1, device_id={"segment": early_seg, "seq": first + step}, device_id_type=MESH
        )

    @pl.loop(1, replicas)
    def _(step):
        pl.semaphore_signal(barrier, 1, device_id=other(step), device_id_type=MESH)

    pl.semaphore_wait(barrier, 2 * group - 1 + replicas - 1)

    @pl.loop(1, replicas)
    def _(step):
        pltpu.make_async_remote_copy(
            src_ref=len_own, dst_ref=len_all.at[own], send_sem=len_send, recv_sem=len_sem,
            device_id=other(step), device_id_type=MESH,
        ).start()

    mem_rows = pl.ds(pl.multiple_of(rank * mem_tokens, mem_tokens), mem_tokens)

    @pl.loop(0, group)
    def _(step):
        to = partner(step)
        lanes = pl.ds(pl.multiple_of(to * owned, owned), owned)
        for pair, (src, dst) in enumerate(((mk_ref, mk_buf), (mv_ref, mv_buf))):
            pltpu.make_async_remote_copy(
                src_ref=src.at[:, lanes], dst_ref=dst.at[mem_rows],
                send_sem=mem_send.at[pair], recv_sem=mem_sem.at[pair],
                device_id={"segment": later_seg, "seq": first + to}, device_id_type=MESH,
            ).start()

    own_lanes = pl.ds(pl.multiple_of(rank * tokens, tokens), tokens)
    kinds = ((dk_ref, k_buf), (dv_ref, v_buf), (dq_ref, q_buf), (cq_ref, c_buf))

    def landing(kind, h):
        shift = h * HS if kind == 3 else 0
        return kinds[kind][1].at[h, pl.ds(shift, HS)]

    for h in range(heads):
        for kind in range(4):
            src = kinds[kind][0]
            dst = landing(kind, h).at[:, own_lanes]
            sem = in_sems.at[h, kind]
            pltpu.make_async_copy(
                src.at[pl.ds(pl.multiple_of(rank * owned, owned) + h * HS, HS)], dst, sem
            ).start()

            @pl.loop(1, group)
            def _(step):
                to = partner(step)
                pltpu.make_async_remote_copy(
                    src_ref=src.at[pl.ds(pl.multiple_of(to * owned, owned) + h * HS, HS)],
                    dst_ref=dst, send_sem=send_sem.at[kind], recv_sem=sem,
                    device_id={"seq": first + to}, device_id_type=MESH,
                ).start()

    pltpu.make_async_copy(len_all.at[pl.ds(1, replicas - 1)], len_all.at[pl.ds(1, replicas - 1)], len_sem).wait()
    live = jnp.sum(len_all[...], axis=0)[0:1]
    scale = jnp.float32(n_seg * n_dp * SEQS * seq_len) / live.astype(jnp.float32)
    scale = jnp.concatenate([scale] * (BLOCK // 128), axis=1)

    pltpu.make_async_copy(mk_buf, mk_buf, mem_sem.at[0]).wait()
    pltpu.make_async_copy(mv_buf, mv_buf, mem_sem.at[1]).wait()
    mem_len = mk_buf.shape[0]
    ones = jnp.where(lax.broadcasted_iota(jnp.int32, (16, mem_len), 0) == 0, 1.0, 0.0).astype(jnp.bfloat16)
    values_t = mv_buf[...].T
    for h in range(heads):
        mvt_buf[h] = jnp.concatenate([values_t[h * HS : (h + 1) * HS], ones], axis=0)
    lane = lax.broadcasted_iota(jnp.int32, (mem_len, owned), 1)
    token = lax.broadcasted_iota(jnp.int32, (mem_len, owned), 0)

    def attend(keys, queries, values, causal):
        scores = jnp.dot(keys, queries, preferred_element_type=jnp.float32)
        if causal:
            rows = scores.shape[0] - BLOCK
            i = lax.broadcasted_iota(jnp.int32, (BLOCK, BLOCK), 1)
            j = lax.broadcasted_iota(jnp.int32, (BLOCK, BLOCK), 0)
            last = jnp.where(j <= i, scores[rows:], MASKED)
            scores = jnp.concatenate([scores[:rows], last], axis=0) if rows else last
        highest = jnp.max(scores, axis=0, keepdims=True)
        weights = jnp.exp(scores - highest).astype(jnp.bfloat16)
        both = jnp.dot(values, weights, preferred_element_type=jnp.float32)
        context = both[:HS] / both[HS : HS + 1]
        return context

    for h in range(heads):
        for kind in range(4):
            sem = in_sems.at[h, kind]
            pltpu.make_async_copy(landing(kind, h), landing(kind, h), sem).wait()
        for j in range(0, seq_len, 128):
            kt_buf[j : j + 128, :] = k_buf[h, :, j : j + 128].T
        inside = (lane >= h * HS) & (lane < (h + 1) * HS)
        mask = jnp.where((lane == (1 - h) * HS) & (token >= source), MASKED, 0.0).astype(jnp.bfloat16)
        mem_keys = jnp.where(inside, mk_buf[...], mask)
        for b in range(seq_len // BLOCK):
            i0 = b * BLOCK
            self_part = attend(
                kt_buf[: i0 + BLOCK, :], q_buf[h, :, i0 : i0 + BLOCK], v_buf[h, :, : i0 + BLOCK], True
            )
            cross_part = attend(mem_keys, c_buf[h, :, i0 : i0 + BLOCK], mvt_buf[h], False)
            position = i0 + lax.broadcasted_iota(jnp.int32, (1, BLOCK), 1)
            weight = jnp.where(position < target, scale, 0.0)
            o_buf[h, :, i0 : i0 + BLOCK] = ((self_part + cross_part) * weight).astype(jnp.bfloat16)
            for to in range(i0 // tokens, (i0 + BLOCK) // tokens):
                src = o_buf.at[h, :, pl.ds(to * tokens, tokens)]
                dst = out_ref.at[pl.ds(pl.multiple_of(rank * owned, owned) + h * HS, HS)]

                @pl.when(rank != to)
                def _():
                    pltpu.make_async_remote_copy(
                        src_ref=src, dst_ref=dst, send_sem=out_send, recv_sem=out_sem,
                        device_id={"seq": first + to}, device_id_type=MESH,
                    ).start()

                @pl.when(rank == to)
                def _():
                    pltpu.make_async_copy(src, dst, out_sem).start()

    def drain(ref, sem):
        pltpu.make_async_copy(ref, ref, sem).wait()

    drain(len_all.at[pl.ds(1, replicas - 1)], len_send)
    drain(mk_buf, mem_send.at[0])
    drain(mv_buf, mem_send.at[1])
    for kind in range(4):
        drain(kinds[kind][1].at[:, pl.ds(0, HS), pl.ds(0, seq_len - tokens)], send_sem.at[kind])
    drain(o_buf.at[:, :, pl.ds(0, seq_len - tokens)], out_send)
    drain(out_ref, out_sem)


def local(n_seg, n_seq, n_dp, dq, dk, dv, cq, mk, mv, target, source):
    features, tokens = dq.shape[2:]
    group = n_seq // SEQS
    seq_len = group * tokens
    owned = features // group
    heads = owned // HS
    mem_tokens = mk.shape[3]
    flat = [a.reshape(features, tokens) for a in (dq, dk, dv, cq)]
    memory = [a.reshape(features, mem_tokens).T for a in (mk, mv)]
    bf16 = jnp.bfloat16
    dma = pltpu.SemaphoreType.DMA
    out = pl.pallas_call(
        functools.partial(kernel, n_seg, n_seq, n_dp),
        out_shape=jax.ShapeDtypeStruct((features, tokens), bf16),
        in_specs=[pl.BlockSpec(memory_space=pltpu.SMEM)] * 2 + [pl.BlockSpec(memory_space=pl.ANY)] * 6,
        out_specs=pl.BlockSpec(memory_space=pl.ANY),
        scratch_shapes=[
            pltpu.VMEM((heads, 2 * HS, seq_len), bf16),
            pltpu.VMEM((heads, 2 * HS, seq_len), bf16),
            pltpu.VMEM((heads, HS + 16, seq_len), bf16),
            pltpu.VMEM((heads, 2 * HS, seq_len), bf16),
            pltpu.VMEM((group * mem_tokens, owned), bf16),
            pltpu.VMEM((group * mem_tokens, owned), bf16),
            pltpu.VMEM((seq_len, 2 * HS), bf16),
            pltpu.VMEM((heads, HS + 16, group * mem_tokens), bf16),
            pltpu.VMEM((heads, HS, seq_len), bf16),
            pltpu.VMEM((8, 128), jnp.int32),
            pltpu.VMEM((n_seg * n_dp, 8, 128), jnp.int32),
            dma((heads, 4)), dma((2,)), dma, dma, dma((4,)), dma((2,)), dma, dma,
        ],
        compiler_params=pltpu.CompilerParams(
            collective_id=0, has_side_effects=True, vmem_limit_bytes=56 * 2**20
        ),
    )(target, source, *flat, *memory)
    return out.reshape(1, 1, features, tokens)


def solution(mesh):
    sizes = [mesh.shape[name] for name in ("segment", "seq", "dp")]
    wide = P("segment", "dp", None, "seq")
    in_specs = (wide,) * 6 + (P("segment", "dp", None),) * 2
    return jax.shard_map(
        functools.partial(local, *sizes), mesh=mesh, in_specs=in_specs, out_specs=wide, check_vma=False
    )
```

```python
import functools

import jax
import jax.numpy as jnp
from jax import lax
from jax.experimental import pallas as pl
from jax.experimental.pallas import tpu as pltpu
from jax.sharding import PartitionSpec as P

HS = 64
SEQS = 2
BLOCK = 256
LANES = 128
MASKED = -1e30
MESH = pl.DeviceIdType.MESH
K, V, QU, Q, C = range(5)


def kernel(
    n_seg, n_seq, n_dp,
    target_ref, source_ref, dq_ref, dk_ref, dv_ref, cq_ref, mk_ref, mv_ref,
    out_ref,
    q_buf, k_buf, v_buf, c_buf, u_buf, rk_buf, rv_buf, mk_buf, mv_buf, kt_buf, mvt_buf,
    o_buf, part_buf, stat_buf, part_in, stat_in, acc_buf, len_own, len_dp, len_ring,
    in_sems, send_sems, relay_sems, relay_sends, mem_sems, mem_sends, part_sems, stat_sems,
    part_send, stat_send, dp_sem, dp_send, ring_sems, ring_sends, out_sem, out_send,
):
    group = n_seq // SEQS
    pair = group // 2
    tokens = dq_ref.shape[1]
    span = pair * tokens
    seq_len = group * tokens
    mem_tokens = mk_ref.shape[0]
    heads = q_buf.shape[0]
    owned = heads * HS
    blocks = span // BLOCK

    seg, place, dp = lax.axis_index("segment"), lax.axis_index("seq"), lax.axis_index("dp")
    which = place // group
    rank = place % group
    first = which * group
    upper = rank // pair
    part = rank % pair
    base = first + upper * pair
    target = target_ref[0, 0, which]
    source = source_ref[0, 0, which]
    later = {"segment": (seg + 1) % n_seg}
    early = {"segment": (seg + n_seg - 1) % n_seg}

    row = lax.broadcasted_iota(jnp.int32, (HS, span), 0)
    column = upper * span + lax.broadcasted_iota(jnp.int32, (HS, span), 1)
    one_row = jnp.where(row == 0, 1.0, 0.0).astype(jnp.bfloat16)
    mask_row = jnp.where((row == 0) & (column >= target), MASKED, 0.0).astype(jnp.bfloat16)
    for h in range(heads):
        q_buf[h, HS:, :] = one_row
        u_buf[h, HS:, :] = one_row
        k_buf[h, HS:, :] = mask_row
        v_buf[h, HS:, :] = one_row[:16]
        c_buf[h, (1 - h % 2) * HS : (2 - h % 2) * HS, :] = one_row
    lens = jnp.full(len_own.shape, target_ref[0, 0, 0] + target_ref[0, 0, 1], jnp.int32)
    len_own[...] = lens
    len_dp[dp] = lens

    barrier = pltpu.get_barrier_semaphore()

    @pl.loop(1, group)
    def _(step):
        pl.semaphore_signal(
            barrier, 1, device_id={"seq": first + (rank + step) % group}, device_id_type=MESH
        )

    for step in range(1, n_dp):
        pl.semaphore_signal(barrier, 1, device_id={"dp": (dp + step) % n_dp}, device_id_type=MESH)
    pl.semaphore_signal(barrier, 1, device_id=early, device_id_type=MESH)
    pl.semaphore_wait(barrier, group - 1 + n_dp - 1 + 1)

    def remote(src, dst, send, recv, device):
        pltpu.make_async_remote_copy(
            src_ref=src, dst_ref=dst, send_sem=send, recv_sem=recv, device_id=device, device_id_type=MESH
        ).start()

    def drain(ref, sem):
        pltpu.make_async_copy(ref, ref, sem).wait()

    def aligned(index, size):
        return pl.ds(pl.multiple_of(index, size), size)

    for step in range(1, n_dp):
        remote(len_own, len_dp.at[dp], dp_send, dp_sem, {"dp": (dp + step) % n_dp})
    for pos, (src, dst) in enumerate(((mk_ref, rk_buf), (mv_ref, rv_buf))):
        remote(src, dst, relay_sends.at[pos], relay_sems.at[pos], later)

    lanes_own = aligned(part * tokens, tokens)
    kinds = {K: (dk_ref, k_buf), V: (dv_ref, v_buf), QU: (dq_ref, u_buf), Q: (dq_ref, q_buf), C: (cq_ref, c_buf)}

    def send_head(h):
        for kind in (K, V, QU, Q, C):
            src, buf = kinds[kind]
            shift = (h % 2) * HS if kind == C else 0
            dst = buf.at[h, pl.ds(shift, HS), lanes_own]
            sem = in_sems.at[h, kind]

            def rows(to):
                return src.at[pl.ds(pl.multiple_of(to * owned, owned) + h * HS, HS)]

            if kind == QU:

                @pl.when(upper == 1)
                def _():
                    @pl.loop(0, pair)
                    def _(step):
                        to = (part + step) % pair
                        remote(rows(to), dst, send_sems.at[kind], sem, {"seq": first + to})

                continue

            pltpu.make_async_copy(rows(part), dst, sem).start()

            @pl.loop(1, pair)
            def _(step):
                to = (part + step) % pair
                remote(rows(to), dst, send_sems.at[kind], sem, {"seq": base + to})

    send_head(0)
    drain(len_dp.at[pl.ds(1, n_dp - 1)], dp_sem)
    len_ring[0] = jnp.sum(len_dp[...], axis=0)
    remote(len_ring.at[0], len_ring.at[1], ring_sends.at[0], ring_sems.at[0], later)
    send_head(1)
    drain(rk_buf, relay_sems.at[0])
    drain(rv_buf, relay_sems.at[1])
    mem_rows = aligned(rank * mem_tokens, mem_tokens)

    def spread(to, move):
        for pos, (src, dst) in enumerate(((rk_buf, mk_buf), (rv_buf, mv_buf))):
            for couple in range(heads // 2):
                start = pl.multiple_of((to % pair) * owned, owned) + couple * LANES
                move(src.at[:, pl.ds(start, LANES)], dst.at[couple, mem_rows], pos)

    spread(rank, lambda src, dst, pos: pltpu.make_async_copy(src, dst, mem_sems.at[pos]).start())

    @pl.loop(1, group)
    def _(step):
        to = (rank + step) % group
        spread(
            to,
            lambda src, dst, pos: remote(src, dst, mem_sends.at[pos], mem_sems.at[pos], {"seq": first + to}),
        )

    for hop in range(1, n_seg):
        drain(len_ring.at[hop], ring_sems.at[hop - 1])
        if hop < n_seg - 1:
            remote(len_ring.at[hop], len_ring.at[hop + 1], ring_sends.at[hop], ring_sems.at[hop], later)
        if hop == 1:
            for h in range(2, heads):
                send_head(h)

    live = jnp.sum(len_ring[...], axis=0)[0:1]
    scale = jnp.float32(n_seg * n_dp * SEQS * seq_len) / live.astype(jnp.float32)
    scale = jnp.concatenate([scale] * (BLOCK // LANES), axis=1)

    def attend(keys, queries, values, causal):
        scores = jnp.dot(keys, queries, preferred_element_type=jnp.float32)
        if causal:
            rows = scores.shape[0] - BLOCK
            i = lax.broadcasted_iota(jnp.int32, (BLOCK, BLOCK), 1)
            j = lax.broadcasted_iota(jnp.int32, (BLOCK, BLOCK), 0)
            last = jnp.where(j <= i, scores[rows:], MASKED)
            scores = jnp.concatenate([scores[:rows], last], axis=0) if rows else last
        highest = jnp.max(scores, axis=0, keepdims=True)
        weights = jnp.exp(scores - highest).astype(jnp.bfloat16)
        both = jnp.dot(values, weights, preferred_element_type=jnp.float32)
        return both[:HS], both[HS : HS + 1], highest

    def causal_block(h, b):
        upto = (b + 1) * BLOCK
        return attend(kt_buf[:upto], q_buf[h, :, b * BLOCK : upto], v_buf[h, :, :upto], True)

    mem_len = mk_buf.shape[1]
    lane = lax.broadcasted_iota(jnp.int32, (mem_len, LANES), 1)
    token = lax.broadcasted_iota(jnp.int32, (mem_len, LANES), 0)
    part_bytes = part_buf.at[0]

    def finish(h, b, self_part, mem_keys):
        i0 = b * BLOCK
        both, summed, _ = attend(mem_keys, c_buf[h, :, i0 : i0 + BLOCK], mvt_buf[h], False)
        position = upper * span + i0 + lax.broadcasted_iota(jnp.int32, (1, BLOCK), 1)
        weight = jnp.where(position < target, scale, 0.0)
        o_buf[h, :, i0 : i0 + BLOCK] = ((self_part + both / summed) * weight).astype(jnp.bfloat16)
        dst = out_ref.at[pl.ds(pl.multiple_of(part * owned + h * HS, HS), HS)]
        for to in range(i0 // tokens, (i0 + BLOCK) // tokens):
            src = o_buf.at[h, :, pl.ds(to * tokens, tokens)]

            @pl.when(part != to)
            def _():
                remote(src, dst, out_send, out_sem, {"seq": base + to})

            @pl.when(part == to)
            def _():
                pltpu.make_async_copy(src, dst, out_sem).start()

    def memory_keys(h):
        side = h % 2
        inside = (lane >= side * HS) & (lane < (side + 1) * HS)
        mask = jnp.where((lane == (1 - side) * HS) & (token >= source), MASKED, 0.0)
        return jnp.where(inside, mk_buf[h // 2], mask.astype(jnp.bfloat16))

    def merge_head(h):
        drain(part_bytes, part_sems.at[h])
        drain(stat_buf.at[0], stat_sems.at[h])
        mem_keys = memory_keys(h)
        for b in range(blocks):
            cols = slice(b * BLOCK, (b + 1) * BLOCK)
            per = BLOCK // LANES

            def stat(ref, at):
                return jnp.concatenate([ref[h, at + b * per + e : at + b * per + e + 1, :] for e in range(per)], axis=1)

            half = stat_buf.shape[1] // 2
            high_u, sum_u = stat(stat_buf, 0), stat(stat_buf, half)
            high_l, sum_l = stat(stat_in, 0), stat(stat_in, half)
            highest = jnp.maximum(high_u, high_l)
            keep_u, keep_l = jnp.exp(high_u - highest), sum_l * jnp.exp(high_l - highest)
            total = sum_u * keep_u + keep_l
            merged = acc_buf[h, :, cols] * (keep_u / total) + part_in[h, :, cols].astype(jnp.float32) * (keep_l / total)
            finish(h, b, merged, mem_keys)

    def put_stat(h, b, highest, summed):
        per = BLOCK // LANES
        half = stat_buf.shape[1] // 2
        for e in range(per):
            cols = slice(e * LANES, (e + 1) * LANES)
            stat_buf[h, b * per + e : b * per + e + 1, :] = highest[:, cols]
            stat_buf[h, half + b * per + e : half + b * per + e + 1, :] = summed[:, cols]

    def wait_input(h, kind):
        drain(part_bytes, in_sems.at[h, kind])

    drain(mk_buf, mem_sems.at[0])
    drain(mv_buf, mem_sems.at[1])
    ones = jnp.where(lax.broadcasted_iota(jnp.int32, (16, mem_len), 0) == 0, 1.0, 0.0).astype(jnp.bfloat16)
    for couple in range(heads // 2):
        values_t = mv_buf[couple].T
        for side in range(2):
            mvt_buf[2 * couple + side] = jnp.concatenate([values_t[side * HS : (side + 1) * HS], ones], axis=0)

    @pl.loop(0, heads)
    def _(h):
        wait_input(h, K)
        wait_input(h, V)
        for j in range(0, span, LANES):
            kt_buf[j : j + LANES, :] = k_buf[h, :, j : j + LANES].T

        @pl.when(upper == 0)
        def _():
            wait_input(h, QU)
            opposite = {"seq": place + pair}
            for b in range(blocks):
                cols = slice(b * BLOCK, (b + 1) * BLOCK)
                both, summed, highest = attend(kt_buf[...], u_buf[h, :, cols], v_buf[h], False)
                part_buf[h, :, cols] = (both / summed).astype(jnp.bfloat16)
                put_stat(h, b, highest, summed)
                span_cols = pl.ds(b * BLOCK, BLOCK)
                remote(part_buf.at[h, :, span_cols], part_in.at[h, :, span_cols], part_send, part_sems.at[h], opposite)
            remote(stat_buf.at[h], stat_in.at[h], stat_send, stat_sems.at[h], opposite)
            wait_input(h, Q)
            wait_input(h, C)
            mem_keys = memory_keys(h)
            for b in range(blocks):
                both, summed, _ = causal_block(h, b)
                finish(h, b, both / summed, mem_keys)

        @pl.when(upper == 1)
        def _():
            wait_input(h, Q)
            wait_input(h, C)
            for b in range(blocks):
                both, summed, highest = causal_block(h, b)
                acc_buf[h, :, b * BLOCK : (b + 1) * BLOCK] = both
                put_stat(h, b, highest, summed)

            @pl.when(h > 0)
            def _():
                merge_head(h - 1)

    @pl.when(upper == 1)
    def _():
        merge_head(heads - 1)
        drain(part_buf, send_sems.at[QU])

    @pl.when(upper == 0)
    def _():
        drain(part_buf, part_send)
        drain(stat_buf, stat_send)

    if n_dp > 1:
        drain(len_dp.at[pl.ds(1, n_dp - 1)], dp_send)
    for hop in range(n_seg - 1):
        drain(len_ring.at[hop], ring_sends.at[hop])
    drain(rk_buf, relay_sends.at[0])
    drain(rv_buf, relay_sends.at[1])
    for pos, buf in enumerate((mk_buf, mv_buf)):
        drain(buf.at[:, pl.ds(0, mem_len - mem_tokens)], mem_sends.at[pos])
    for kind in (K, V, Q, C):
        drain(part_buf.at[:, :, pl.ds(0, span - tokens)], send_sems.at[kind])
    drain(o_buf.at[:, :, pl.ds(0, span - tokens)], out_send)
    drain(out_ref, out_sem)


def local(n_seg, n_seq, n_dp, dq, dk, dv, cq, mk, mv, target, source):
    features, tokens = dq.shape[2:]
    group = n_seq // SEQS
    pair = group // 2
    span = pair * tokens
    owned = features // pair
    heads = owned // HS
    mem_tokens = mk.shape[3]
    mem_len = group * mem_tokens
    flat = [a.reshape(features, tokens) for a in (dq, dk, dv, cq)]
    memory = [a.reshape(features, mem_tokens).T for a in (mk, mv)]
    bf16, f32, i32 = jnp.bfloat16, jnp.float32, jnp.int32
    dma = pltpu.SemaphoreType.DMA
    wide = pltpu.VMEM((heads, 2 * HS, span), bf16)
    block = pltpu.VMEM((heads, HS, span), bf16)
    stats = pltpu.VMEM((heads, 2 * span // LANES, LANES), f32)
    relay = pltpu.VMEM((mem_tokens, features), bf16)
    memories = pltpu.VMEM((heads // 2, mem_len, LANES), bf16)
    out = pl.pallas_call(
        functools.partial(kernel, n_seg, n_seq, n_dp),
        out_shape=jax.ShapeDtypeStruct((features, tokens), bf16),
        in_specs=[pl.BlockSpec(memory_space=pltpu.SMEM)] * 2 + [pl.BlockSpec(memory_space=pl.ANY)] * 6,
        out_specs=pl.BlockSpec(memory_space=pl.ANY),
        scratch_shapes=[
            wide, wide, pltpu.VMEM((heads, HS + 16, span), bf16), wide, wide,
            relay, relay, memories, memories,
            pltpu.VMEM((span, 2 * HS), bf16),
            pltpu.VMEM((heads, HS + 16, mem_len), bf16),
            block, block, stats, block, stats,
            pltpu.VMEM((heads, HS, span), f32),
            pltpu.VMEM((8, LANES), i32),
            pltpu.VMEM((n_dp, 8, LANES), i32),
            pltpu.VMEM((n_seg, 8, LANES), i32),
            dma((heads, 5)), dma((5,)), dma((2,)), dma((2,)), dma((2,)), dma((2,)), dma((heads,)), dma((heads,)),
            dma, dma, dma, dma, dma((n_seg,)), dma((n_seg,)), dma, dma,
        ],
        compiler_params=pltpu.CompilerParams(
            collective_id=0, has_side_effects=True, vmem_limit_bytes=56 * 2**20
        ),
    )(target, source, *flat, *memory)
    return out.reshape(1, 1, features, tokens)


def solution(mesh):
    sizes = [mesh.shape[name] for name in ("segment", "seq", "dp")]
    wide = P("segment", "dp", None, "seq")
    in_specs = (wide,) * 6 + (P("segment", "dp", None),) * 2
    return jax.shard_map(
        functools.partial(local, *sizes), mesh=mesh, in_specs=in_specs, out_specs=wide, check_vma=False
    )
```

```python
import functools

import jax
import jax.numpy as jnp
from jax import lax
from jax.experimental import pallas as pl
from jax.experimental.pallas import tpu as pltpu
from jax.sharding import PartitionSpec as P

HS = 64
SEQS = 2
BLOCK = 512
LANES = 128
MASKED = -1e30
MESH = pl.DeviceIdType.MESH
K, V, QU, Q, C = range(5)


def kernel(
    n_seg, n_seq, n_dp,
    target_ref, source_ref, dq_ref, dk_ref, dv_ref, cq_ref, mk_ref, mv_ref,
    out_ref,
    q_buf, k_buf, v_buf, c_buf, u_buf, rk_buf, rv_buf, mk_buf, mv_buf, kt_buf, mvt_buf,
    o_buf, part_buf, stat_buf, part_in, stat_in, acc_buf, cross_buf, len_own, len_dp, len_ring,
    in_sems, send_sems, relay_sems, relay_sends, mem_sems, mem_sends, part_sems, stat_sems,
    part_send, stat_send, dp_sem, dp_send, ring_sems, ring_sends, out_sem, out_send,
):
    group = n_seq // SEQS
    pair = group // 2
    tokens = dq_ref.shape[1]
    span = pair * tokens
    seq_len = group * tokens
    mem_tokens = mk_ref.shape[0]
    heads = q_buf.shape[0]
    owned = heads * HS
    blocks = span // BLOCK
    per = span // LANES

    seg, place, dp = lax.axis_index("segment"), lax.axis_index("seq"), lax.axis_index("dp")
    which = place // group
    rank = place % group
    first = which * group
    upper = rank // pair
    part = rank % pair
    base = first + upper * pair
    target = target_ref[0, 0, which]
    source = source_ref[0, 0, which]
    later = {"segment": (seg + 1) % n_seg}
    early = {"segment": (seg + n_seg - 1) % n_seg}

    barrier = pltpu.get_barrier_semaphore()

    @pl.loop(1, group)
    def _(step):
        pl.semaphore_signal(
            barrier, 1, device_id={"seq": first + (rank + step) % group}, device_id_type=MESH
        )

    for step in range(1, n_dp):
        pl.semaphore_signal(barrier, 1, device_id={"dp": (dp + step) % n_dp}, device_id_type=MESH)
    pl.semaphore_signal(barrier, 1, device_id=early, device_id_type=MESH)

    row = lax.broadcasted_iota(jnp.int32, (HS, span), 0)
    column = upper * span + lax.broadcasted_iota(jnp.int32, (HS, span), 1)
    one_row = jnp.where(row == 0, 1.0, 0.0).astype(jnp.bfloat16)
    mask_row = jnp.where((row == 0) & (column >= target), MASKED, 0.0).astype(jnp.bfloat16)
    for h in range(heads):
        q_buf[h, HS:, :] = one_row
        u_buf[h, HS:, :] = one_row
        k_buf[h, HS:, :] = mask_row
        v_buf[h, HS:, :] = one_row[:16]
        c_buf[h, (1 - h % 2) * HS : (2 - h % 2) * HS, :] = one_row
    lens = jnp.full(len_own.shape, target_ref[0, 0, 0] + target_ref[0, 0, 1], jnp.int32)
    len_own[...] = lens
    len_dp[dp] = lens

    pl.semaphore_wait(barrier, group - 1 + n_dp - 1 + 1)

    def remote(src, dst, send, recv, device):
        pltpu.make_async_remote_copy(
            src_ref=src, dst_ref=dst, send_sem=send, recv_sem=recv, device_id=device, device_id_type=MESH
        ).start()

    def drain(ref, sem):
        pltpu.make_async_copy(ref, ref, sem).wait()

    def aligned(start, size):
        return pl.ds(pl.multiple_of(start, size), size)

    for step in range(1, n_dp):
        remote(len_own, len_dp.at[dp], dp_send, dp_sem, {"dp": (dp + step) % n_dp})
    for pos, (src, dst) in enumerate(((mk_ref, rk_buf), (mv_ref, rv_buf))):
        remote(src, dst, relay_sends.at[pos], relay_sems.at[pos], later)

    lanes_own = aligned(part * tokens, tokens)
    kinds = {K: (dk_ref, k_buf), V: (dv_ref, v_buf), QU: (dq_ref, u_buf), Q: (dq_ref, q_buf), C: (cq_ref, c_buf)}

    def send_head(h, which_kinds):
        for kind in which_kinds:
            src, buf = kinds[kind]
            shift = (h % 2) * HS if kind == C else 0
            dst = buf.at[h, pl.ds(shift, HS), lanes_own]
            sem = in_sems.at[h, kind]

            def rows(to):
                return src.at[pl.ds(pl.multiple_of(to * owned, owned) + h * HS, HS)]

            if kind == QU:

                @pl.when(upper == 1)
                def _():
                    @pl.loop(0, pair)
                    def _(step):
                        to = (part + step) % pair
                        remote(rows(to), dst, send_sems.at[kind], sem, {"seq": first + to})

                continue

            pltpu.make_async_copy(rows(part), dst, sem).start()

            @pl.loop(1, pair)
            def _(step):
                to = (part + step) % pair
                remote(rows(to), dst, send_sems.at[kind], sem, {"seq": base + to})

    first_kinds, last_kinds = (K, V, QU), (Q, C)
    send_head(0, first_kinds)
    drain(len_dp.at[pl.ds(1, n_dp - 1)], dp_sem)
    len_ring[0] = jnp.sum(len_dp[...], axis=0)
    remote(len_ring.at[0], len_ring.at[1], ring_sends.at[0], ring_sems.at[0], later)
    send_head(1, first_kinds)
    send_head(0, last_kinds)
    drain(rk_buf, relay_sems.at[0])
    drain(rv_buf, relay_sems.at[1])
    mem_rows = aligned(rank * mem_tokens, mem_tokens)

    def spread(to, move):
        for pos, (src, dst) in enumerate(((rk_buf, mk_buf), (rv_buf, mv_buf))):
            for couple in range(heads // 2):
                start = pl.multiple_of((to % pair) * owned, owned) + couple * LANES
                move(src.at[:, pl.ds(start, LANES)], dst.at[couple, mem_rows], pos)

    spread(rank, lambda src, dst, pos: pltpu.make_async_copy(src, dst, mem_sems.at[pos]).start())

    @pl.loop(1, group)
    def _(step):
        to = (rank + step) % group
        spread(
            to,
            lambda src, dst, pos: remote(src, dst, mem_sends.at[pos], mem_sems.at[pos], {"seq": first + to}),
        )

    for hop in range(1, n_seg):
        drain(len_ring.at[hop], ring_sems.at[hop - 1])
        if hop < n_seg - 1:
            remote(len_ring.at[hop], len_ring.at[hop + 1], ring_sends.at[hop], ring_sems.at[hop], later)
        if hop == 1:
            for h in range(2, heads):
                send_head(h, first_kinds)
                send_head(h - 1, last_kinds)
            send_head(heads - 1, last_kinds)

    live = jnp.sum(len_ring[...], axis=0)[0:1]
    scale = jnp.float32(n_seg * n_dp * SEQS * seq_len) / live.astype(jnp.float32)
    position = upper * span + lax.broadcasted_iota(jnp.int32, (1, span), 1)
    weight = jnp.where(position < target, jnp.concatenate([scale] * per, axis=1), 0.0)

    def attend(keys, queries, values, causal):
        scores = jnp.dot(keys, queries, preferred_element_type=jnp.float32)
        if causal:
            rows = scores.shape[0] - BLOCK
            i = lax.broadcasted_iota(jnp.int32, (BLOCK, BLOCK), 1)
            j = lax.broadcasted_iota(jnp.int32, (BLOCK, BLOCK), 0)
            last = jnp.where(j <= i, scores[rows:], MASKED)
            scores = jnp.concatenate([scores[:rows], last], axis=0) if rows else last
        highest = jnp.max(scores, axis=0, keepdims=True)
        weights = jnp.exp(scores - highest).astype(jnp.bfloat16)
        both = jnp.dot(values, weights, preferred_element_type=jnp.float32)
        return both[:HS], both[HS : HS + 1], highest

    def causal_block(h, b):
        upto = (b + 1) * BLOCK
        return attend(kt_buf[h, :upto], q_buf[h, :, b * BLOCK : upto], v_buf[h, :, :upto], True)

    mem_len = mk_buf.shape[1]
    lane = lax.broadcasted_iota(jnp.int32, (mem_len, LANES), 1)
    token = lax.broadcasted_iota(jnp.int32, (mem_len, LANES), 0)
    part_bytes = part_buf.at[0]

    def finish(h, self_part, cross_part):
        o_buf[h] = ((self_part + cross_part) * weight).astype(jnp.bfloat16)
        dst = out_ref.at[pl.ds(pl.multiple_of(part * owned + h * HS, HS), HS)]
        pltpu.make_async_copy(o_buf.at[h, :, lanes_own], dst, out_sem).start()

        @pl.loop(1, pair)
        def _(step):
            to = (part + step) % pair
            remote(o_buf.at[h, :, aligned(to * tokens, tokens)], dst, out_send, out_sem, {"seq": base + to})

    def cross(h):
        both, summed, _ = attend(memory_keys(h), c_buf[h], mvt_buf[h], False)
        return both / summed

    def causal(h):
        pieces = [causal_block(h, b) for b in range(blocks)]
        return [jnp.concatenate([piece[k] for piece in pieces], axis=1) for k in range(3)]

    def memory_keys(h):
        side = h % 2
        inside = (lane >= side * HS) & (lane < (side + 1) * HS)
        mask = jnp.where((lane == (1 - side) * HS) & (token >= source), MASKED, 0.0)
        return jnp.where(inside, mk_buf[h // 2], mask.astype(jnp.bfloat16))

    def put_stat(h, highest, summed):
        for e in range(per):
            cols = slice(e * LANES, (e + 1) * LANES)
            stat_buf[h, e : e + 1, :] = highest[:, cols]
            stat_buf[h, per + e : per + e + 1, :] = summed[:, cols]

    def get_stat(ref, h):
        wide = [jnp.concatenate([ref[h, at + e : at + e + 1, :] for e in range(per)], axis=1) for at in (0, per)]
        return wide

    def merge_head(h):
        drain(part_bytes, part_sems.at[h])
        drain(stat_buf.at[0], stat_sems.at[h])
        high_u, sum_u = get_stat(stat_buf, h)
        high_l, sum_l = get_stat(stat_in, h)
        highest = jnp.maximum(high_u, high_l)
        keep_u, keep_l = jnp.exp(high_u - highest), sum_l * jnp.exp(high_l - highest)
        total = sum_u * keep_u + keep_l
        merged = acc_buf[h] * (keep_u / total) + part_in[h].astype(jnp.float32) * (keep_l / total)
        finish(h, merged, cross_buf[h])

    def wait_input(h, kind):
        drain(part_bytes, in_sems.at[h, kind])

    drain(mk_buf, mem_sems.at[0])
    drain(mv_buf, mem_sems.at[1])
    ones = jnp.where(lax.broadcasted_iota(jnp.int32, (16, mem_len), 0) == 0, 1.0, 0.0).astype(jnp.bfloat16)
    for couple in range(heads // 2):
        values_t = mv_buf[couple].T
        for side in range(2):
            mvt_buf[2 * couple + side] = jnp.concatenate([values_t[side * HS : (side + 1) * HS], ones], axis=0)

    def take_keys(h):
        wait_input(h, K)
        wait_input(h, V)
        for j in range(0, span, LANES):
            kt_buf[h, j : j + LANES, :] = k_buf[h, :, j : j + LANES].T

    @pl.when(upper == 0)
    def _():
        opposite = {"seq": place + pair}

        @pl.loop(0, heads + 1)
        def _(step):
            @pl.when(step < heads)
            def _():
                h = step
                take_keys(h)
                wait_input(h, QU)
                both, summed, highest = attend(kt_buf[h], u_buf[h], v_buf[h], False)
                part_buf[h] = (both / summed).astype(jnp.bfloat16)
                put_stat(h, highest, summed)
                remote(part_buf.at[h], part_in.at[h], part_send, part_sems.at[h], opposite)
                remote(stat_buf.at[h], stat_in.at[h], stat_send, stat_sems.at[h], opposite)

            @pl.when(step > 0)
            def _():
                h = step - 1
                wait_input(h, Q)
                wait_input(h, C)
                both, summed, _ = causal(h)
                finish(h, both / summed, cross(h))

    @pl.when(upper == 1)
    def _():
        @pl.loop(0, heads)
        def _(h):
            take_keys(h)
            wait_input(h, Q)
            wait_input(h, C)
            both, summed, highest = causal(h)
            acc_buf[h] = both
            put_stat(h, highest, summed)
            cross_buf[h] = cross(h)

            @pl.when(h > 0)
            def _():
                merge_head(h - 1)

    @pl.when(upper == 1)
    def _():
        merge_head(heads - 1)
        drain(part_buf, send_sems.at[QU])

    @pl.when(upper == 0)
    def _():
        drain(part_buf, part_send)
        drain(stat_buf, stat_send)

    if n_dp > 1:
        drain(len_dp.at[pl.ds(1, n_dp - 1)], dp_send)
    for hop in range(n_seg - 1):
        drain(len_ring.at[hop], ring_sends.at[hop])
    drain(rk_buf, relay_sends.at[0])
    drain(rv_buf, relay_sends.at[1])
    for pos, buf in enumerate((mk_buf, mv_buf)):
        drain(buf.at[:, pl.ds(0, mem_len - mem_tokens)], mem_sends.at[pos])
    for kind in (K, V, Q, C):
        drain(part_buf.at[:, :, pl.ds(0, span - tokens)], send_sems.at[kind])
    drain(o_buf.at[:, :, pl.ds(0, span - tokens)], out_send)
    drain(out_ref, out_sem)


def local(n_seg, n_seq, n_dp, dq, dk, dv, cq, mk, mv, target, source):
    features, tokens = dq.shape[2:]
    group = n_seq // SEQS
    pair = group // 2
    span = pair * tokens
    owned = features // pair
    heads = owned // HS
    mem_tokens = mk.shape[3]
    mem_len = group * mem_tokens
    flat = [a.reshape(features, tokens) for a in (dq, dk, dv, cq)]
    memory = [a.reshape(features, mem_tokens).T for a in (mk, mv)]
    bf16, f32, i32 = jnp.bfloat16, jnp.float32, jnp.int32
    dma = pltpu.SemaphoreType.DMA
    wide = pltpu.VMEM((heads, 2 * HS, span), bf16)
    block = pltpu.VMEM((heads, HS, span), bf16)
    stats = pltpu.VMEM((heads, 2 * span // LANES, LANES), f32)
    relay = pltpu.VMEM((mem_tokens, features), bf16)
    memories = pltpu.VMEM((heads // 2, mem_len, LANES), bf16)
    out = pl.pallas_call(
        functools.partial(kernel, n_seg, n_seq, n_dp),
        out_shape=jax.ShapeDtypeStruct((features, tokens), bf16),
        in_specs=[pl.BlockSpec(memory_space=pltpu.SMEM)] * 2 + [pl.BlockSpec(memory_space=pl.ANY)] * 6,
        out_specs=pl.BlockSpec(memory_space=pltpu.VMEM),
        scratch_shapes=[
            wide, wide, pltpu.VMEM((heads, HS + 16, span), bf16), wide, wide,
            relay, relay, memories, memories,
            pltpu.VMEM((heads, span, 2 * HS), bf16),
            pltpu.VMEM((heads, HS + 16, mem_len), bf16),
            block, block, stats, block, stats,
            pltpu.VMEM((heads, HS, span), f32),
            pltpu.VMEM((heads, HS, span), f32),
            pltpu.VMEM((8, LANES), i32),
            pltpu.VMEM((n_dp, 8, LANES), i32),
            pltpu.VMEM((n_seg, 8, LANES), i32),
            dma((heads, 5)), dma((5,)), dma((2,)), dma((2,)), dma((2,)), dma((2,)), dma((heads,)), dma((heads,)),
            dma, dma, dma, dma, dma((n_seg,)), dma((n_seg,)), dma, dma,
        ],
        compiler_params=pltpu.CompilerParams(
            collective_id=0, has_side_effects=True, vmem_limit_bytes=56 * 2**20
        ),
    )(target, source, *flat, *memory)
    return out.reshape(1, 1, features, tokens)


def solution(mesh):
    sizes = [mesh.shape[name] for name in ("segment", "seq", "dp")]
    wide = P("segment", "dp", None, "seq")
    in_specs = (wide,) * 6 + (P("segment", "dp", None),) * 2
    return jax.shard_map(
        functools.partial(local, *sizes), mesh=mesh, in_specs=in_specs, out_specs=wide, check_vma=False
    )
```

```python
import functools

import jax
import jax.numpy as jnp
from jax import lax
from jax.experimental import pallas as pl
from jax.experimental.pallas import tpu as pltpu
from jax.sharding import PartitionSpec as P

HS = 64
SEQS = 2
BLOCK = 512
LANES = 128
MASKED = -1e30
MESH = pl.DeviceIdType.MESH
K, V, QU, Q, C = range(5)


def kernel(
    n_seg, n_seq, n_dp,
    target_ref, source_ref, dq_ref, dk_ref, dv_ref, cq_ref, mk_ref, mv_ref,
    out_ref,
    q_buf, k_buf, v_buf, c_buf, u_buf, rk_buf, rv_buf, mk_buf, mv_buf, kt_buf, mvt_buf,
    o_buf, part_buf, stat_buf, part_in, stat_in, acc_buf, weight_buf, len_own, len_dp, len_ring,
    in_sems, send_sems, relay_sems, relay_sends, mem_sems, mem_sends, part_sems, stat_sems,
    part_send, stat_send, dp_sems, dp_send, ready_sem, ring_sems, ring_sends, out_sem, out_send,
):
    group = n_seq // SEQS
    pair = group // 2
    tokens = dq_ref.shape[1]
    span = pair * tokens
    seq_len = group * tokens
    mem_tokens = mk_ref.shape[0]
    heads = q_buf.shape[0]
    owned = heads * HS
    blocks = span // BLOCK
    per = span // LANES

    seg, place, dp = lax.axis_index("segment"), lax.axis_index("seq"), lax.axis_index("dp")
    which = place // group
    rank = place % group
    first = which * group
    upper = rank // pair
    part = rank % pair
    base = first + upper * pair
    target = target_ref[0, 0, which]
    source = source_ref[0, 0, which]
    later = {"segment": (seg + 1) % n_seg}
    early = {"segment": (seg + n_seg - 1) % n_seg}

    barrier = pltpu.get_barrier_semaphore()

    @pl.loop(1, group)
    def _(step):
        pl.semaphore_signal(
            barrier, 1, device_id={"seq": first + (rank + step) % group}, device_id_type=MESH
        )

    order = (dp % 2) * (n_dp // 2) + dp // 2

    def dp_at(turn):
        return {"dp": (turn % 2) * (n_dp // 2) + turn // 2}

    for turn in range(1, n_dp):

        @pl.when(turn > order)
        def _():
            pl.semaphore_signal(barrier, 1, device_id=dp_at(turn), device_id_type=MESH)

    @pl.when(seg < n_seg - 1)
    def _():
        pl.semaphore_signal(barrier, 1, device_id=later, device_id_type=MESH)

    @pl.when(seg == 0)
    def _():
        pl.semaphore_signal(barrier, 1, device_id=early, device_id_type=MESH)


    row = lax.broadcasted_iota(jnp.int32, (HS, span), 0)
    column = upper * span + lax.broadcasted_iota(jnp.int32, (HS, span), 1)
    one_row = jnp.where(row == 0, 1.0, 0.0).astype(jnp.bfloat16)
    mask_row = jnp.where((row == 0) & (column >= target), MASKED, 0.0).astype(jnp.bfloat16)
    for h in range(heads):
        q_buf[h, HS:, :] = one_row
        u_buf[h, HS:, :] = one_row
        k_buf[h, HS:, :] = mask_row
        v_buf[h, HS:, :] = one_row[:16]
        c_buf[h, (1 - h % 2) * HS : (2 - h % 2) * HS, :] = one_row
    lens = jnp.full(len_own.shape, target_ref[0, 0, 0] + target_ref[0, 0, 1], jnp.int32)
    len_own[...] = lens
    len_dp[order] = lens

    first_here = jnp.where(seg > 0, 1, 0) + jnp.where(seg == n_seg - 1, 1, 0)
    pl.semaphore_wait(barrier, group - 1 + order + first_here)

    @pl.when(seg > 0)
    def _():
        pl.semaphore_signal(ready_sem, 1, device_id=early, device_id_type=MESH)

    def remote(src, dst, send, recv, device):
        pltpu.make_async_remote_copy(
            src_ref=src, dst_ref=dst, send_sem=send, recv_sem=recv, device_id=device, device_id_type=MESH
        ).start()

    def drain(ref, sem):
        pltpu.make_async_copy(ref, ref, sem).wait()

    def aligned(start, size):
        return pl.ds(pl.multiple_of(start, size), size)

    def send_lengths(turn):
        remote(len_own, len_dp.at[order], dp_send, dp_sems.at[order], dp_at(turn))

    def take_lengths(turn):
        drain(len_dp.at[turn], dp_sems.at[turn])

    for turn in range(n_dp - 1):

        @pl.when(turn < order)
        def _():
            send_lengths(turn)

    lanes_own = aligned(part * tokens, tokens)
    kinds = {K: (dk_ref, k_buf), V: (dv_ref, v_buf), QU: (dq_ref, u_buf), Q: (dq_ref, q_buf), C: (cq_ref, c_buf)}

    def send_head(h, which_kinds):
        for kind in which_kinds:
            src, buf = kinds[kind]
            shift = (h % 2) * HS if kind == C else 0
            dst = buf.at[h, pl.ds(shift, HS), lanes_own]
            sem = in_sems.at[h, kind]

            def rows(to):
                return src.at[pl.ds(pl.multiple_of(to * owned, owned) + h * HS, HS)]

            if kind == QU:

                @pl.when(upper == 1)
                def _():
                    @pl.loop(0, pair)
                    def _(step):
                        to = (part + step) % pair
                        remote(rows(to), dst, send_sems.at[kind], sem, {"seq": first + to})

                continue

            pltpu.make_async_copy(rows(part), dst, sem).start()

            @pl.loop(1, pair)
            def _(step):
                to = (part + step) % pair
                remote(rows(to), dst, send_sems.at[kind], sem, {"seq": base + to})

    first_kinds, last_kinds = (K, V, QU), (Q, C)
    send_head(0, first_kinds)
    send_head(1, first_kinds)
    send_head(0, last_kinds)

    @pl.when(seg < n_seg - 1)
    def _():
        pl.semaphore_wait(ready_sem, 1)

    for pos, (src, dst) in enumerate(((mk_ref, rk_buf), (mv_ref, rv_buf))):
        remote(src, dst, relay_sends.at[pos], relay_sems.at[pos], later)
    send_head(2, first_kinds)
    send_head(1, last_kinds)
    for turn in range(1, n_dp):

        @pl.when(turn > order)
        def _():
            take_lengths(turn)
            send_lengths(turn)

    for turn in range(n_dp - 1):

        @pl.when(turn < order)
        def _():
            take_lengths(turn)

    len_ring[0] = jnp.sum(len_dp[...], axis=0)
    remote(len_ring.at[0], len_ring.at[1], ring_sends.at[0], ring_sems.at[0], later)

    def pass_lengths(hop):
        drain(len_ring.at[hop], ring_sems.at[hop - 1])
        if hop < n_seg - 1:
            remote(len_ring.at[hop], len_ring.at[hop + 1], ring_sends.at[hop], ring_sems.at[hop], later)

    drain(rk_buf, relay_sems.at[0])
    drain(rv_buf, relay_sems.at[1])
    mem_rows = aligned(rank * mem_tokens, mem_tokens)

    def spread(to, move):
        for pos, (src, dst) in enumerate(((rk_buf, mk_buf), (rv_buf, mv_buf))):
            for couple in range(heads // 2):
                start = pl.multiple_of((to % pair) * owned, owned) + couple * LANES
                move(src.at[:, pl.ds(start, LANES)], dst.at[couple, mem_rows], pos)

    spread(rank, lambda src, dst, pos: pltpu.make_async_copy(src, dst, mem_sems.at[pos]).start())

    @pl.loop(1, group)
    def _(step):
        to = (rank + step) % group
        spread(
            to,
            lambda src, dst, pos: remote(src, dst, mem_sends.at[pos], mem_sems.at[pos], {"seq": first + to}),
        )

    for h in range(3, heads):
        send_head(h, first_kinds)
        send_head(h - 1, last_kinds)
    send_head(heads - 1, last_kinds)
    pass_lengths(1)

    def attend(keys, queries, values, causal):
        scores = jnp.dot(keys, queries, preferred_element_type=jnp.float32)
        if causal:
            rows = scores.shape[0] - BLOCK
            i = lax.broadcasted_iota(jnp.int32, (BLOCK, BLOCK), 1)
            j = lax.broadcasted_iota(jnp.int32, (BLOCK, BLOCK), 0)
            last = jnp.where(j <= i, scores[rows:], MASKED)
            scores = jnp.concatenate([scores[:rows], last], axis=0) if rows else last
        highest = jnp.max(scores, axis=0, keepdims=True)
        weights = jnp.exp(scores - highest).astype(jnp.bfloat16)
        both = jnp.dot(values, weights, preferred_element_type=jnp.float32)
        return both[:HS], both[HS : HS + 1], highest

    def causal_block(h, b):
        upto = (b + 1) * BLOCK
        return attend(kt_buf[h, :upto], q_buf[h, :, b * BLOCK : upto], v_buf[h, :, :upto], True)

    mem_len = mk_buf.shape[1]
    lane = lax.broadcasted_iota(jnp.int32, (mem_len, LANES), 1)
    token = lax.broadcasted_iota(jnp.int32, (mem_len, LANES), 0)
    part_bytes = part_buf.at[0]

    def finish(h, self_part, cross_part):
        o_buf[h] = ((self_part + cross_part) * weight_buf[...]).astype(jnp.bfloat16)
        dst = out_ref.at[pl.ds(pl.multiple_of(part * owned + h * HS, HS), HS)]
        pltpu.make_async_copy(o_buf.at[h, :, lanes_own], dst, out_sem).start()

        @pl.loop(1, pair)
        def _(step):
            to = (part + step) % pair
            remote(o_buf.at[h, :, aligned(to * tokens, tokens)], dst, out_send, out_sem, {"seq": base + to})

    def cross(h):
        both, summed, _ = attend(memory_keys(h), c_buf[h], mvt_buf[h], False)
        return both / summed

    def causal(h):
        pieces = [causal_block(h, b) for b in range(blocks)]
        return [jnp.concatenate([piece[k] for piece in pieces], axis=1) for k in range(3)]

    def memory_keys(h):
        side = h % 2
        inside = (lane >= side * HS) & (lane < (side + 1) * HS)
        mask = jnp.where((lane == (1 - side) * HS) & (token >= source), MASKED, 0.0)
        return jnp.where(inside, mk_buf[h // 2], mask.astype(jnp.bfloat16))

    def put_stat(h, highest, summed):
        for e in range(per):
            cols = slice(e * LANES, (e + 1) * LANES)
            stat_buf[h, e : e + 1, :] = highest[:, cols]
            stat_buf[h, per + e : per + e + 1, :] = summed[:, cols]

    def get_stat(ref, h):
        wide = [jnp.concatenate([ref[h, at + e : at + e + 1, :] for e in range(per)], axis=1) for at in (0, per)]
        return wide

    def merge_head(h):
        wait_input(h, C)
        cross_part = cross(h)
        drain(part_bytes, part_sems.at[h])
        drain(stat_buf.at[0], stat_sems.at[h])
        high_u, sum_u = get_stat(stat_buf, h)
        high_l, sum_l = get_stat(stat_in, h)
        highest = jnp.maximum(high_u, high_l)
        keep_u, keep_l = jnp.exp(high_u - highest), sum_l * jnp.exp(high_l - highest)
        total = sum_u * keep_u + keep_l
        merged = acc_buf[h] * (keep_u / total) + part_in[h].astype(jnp.float32) * (keep_l / total)
        finish(h, merged, cross_part)

    def wait_input(h, kind):
        drain(part_bytes, in_sems.at[h, kind])

    def take_memory():
        for hop in range(2, n_seg):
            pass_lengths(hop)
        live = jnp.sum(len_ring[...], axis=0)[0:1]
        scale = jnp.float32(n_seg * n_dp * SEQS * seq_len) / live.astype(jnp.float32)
        position = upper * span + lax.broadcasted_iota(jnp.int32, (1, span), 1)
        weight_buf[...] = jnp.where(position < target, jnp.concatenate([scale] * per, axis=1), 0.0)
        drain(mk_buf, mem_sems.at[0])
        drain(mv_buf, mem_sems.at[1])
        ones = jnp.where(lax.broadcasted_iota(jnp.int32, (16, mem_len), 0) == 0, 1.0, 0.0).astype(jnp.bfloat16)
        for couple in range(heads // 2):
            values_t = mv_buf[couple].T
            for side in range(2):
                mvt_buf[2 * couple + side] = jnp.concatenate([values_t[side * HS : (side + 1) * HS], ones], axis=0)

    def take_keys(h):
        wait_input(h, K)
        wait_input(h, V)
        for j in range(0, span, LANES):
            kt_buf[h, j : j + LANES, :] = k_buf[h, :, j : j + LANES].T

    @pl.when(upper == 0)
    def _():
        opposite = {"seq": place + pair}

        @pl.loop(0, heads + 1)
        def _(step):
            @pl.when(step < heads)
            def _():
                h = step
                take_keys(h)
                wait_input(h, QU)
                both, summed, highest = attend(kt_buf[h], u_buf[h], v_buf[h], False)
                part_buf[h] = (both / summed).astype(jnp.bfloat16)
                put_stat(h, highest, summed)
                remote(part_buf.at[h], part_in.at[h], part_send, part_sems.at[h], opposite)
                remote(stat_buf.at[h], stat_in.at[h], stat_send, stat_sems.at[h], opposite)

            @pl.when(step == 1)
            def _():
                take_memory()

            @pl.when(step > 0)
            def _():
                h = step - 1
                wait_input(h, Q)
                wait_input(h, C)
                both, summed, _ = causal(h)
                finish(h, both / summed, cross(h))

    @pl.when(upper == 1)
    def _():
        @pl.loop(0, heads)
        def _(h):
            take_keys(h)
            wait_input(h, Q)
            both, summed, highest = causal(h)
            acc_buf[h] = both
            put_stat(h, highest, summed)

            @pl.when(h == 1)
            def _():
                take_memory()

            @pl.when(h > 0)
            def _():
                merge_head(h - 1)

    @pl.when(upper == 1)
    def _():
        merge_head(heads - 1)
        drain(part_buf, send_sems.at[QU])

    @pl.when(upper == 0)
    def _():
        drain(part_buf, part_send)
        drain(stat_buf, stat_send)

    if n_dp > 1:
        drain(len_dp.at[pl.ds(1, n_dp - 1)], dp_send)
    for hop in range(n_seg - 1):
        drain(len_ring.at[hop], ring_sends.at[hop])
    drain(rk_buf, relay_sends.at[0])
    drain(rv_buf, relay_sends.at[1])
    for pos, buf in enumerate((mk_buf, mv_buf)):
        drain(buf.at[:, pl.ds(0, mem_len - mem_tokens)], mem_sends.at[pos])
    for kind in (K, V, Q, C):
        drain(part_buf.at[:, :, pl.ds(0, span - tokens)], send_sems.at[kind])
    drain(o_buf.at[:, :, pl.ds(0, span - tokens)], out_send)
    drain(out_ref, out_sem)


def local(n_seg, n_seq, n_dp, dq, dk, dv, cq, mk, mv, target, source):
    features, tokens = dq.shape[2:]
    group = n_seq // SEQS
    pair = group // 2
    span = pair * tokens
    owned = features // pair
    heads = owned // HS
    mem_tokens = mk.shape[3]
    mem_len = group * mem_tokens
    flat = [a.reshape(features, tokens) for a in (dq, dk, dv, cq)]
    memory = [a.reshape(features, mem_tokens).T for a in (mk, mv)]
    bf16, f32, i32 = jnp.bfloat16, jnp.float32, jnp.int32
    dma = pltpu.SemaphoreType.DMA
    wide = pltpu.VMEM((heads, 2 * HS, span), bf16)
    block = pltpu.VMEM((heads, HS, span), bf16)
    stats = pltpu.VMEM((heads, 2 * span // LANES, LANES), f32)
    relay = pltpu.VMEM((mem_tokens, features), bf16)
    memories = pltpu.VMEM((heads // 2, mem_len, LANES), bf16)
    out = pl.pallas_call(
        functools.partial(kernel, n_seg, n_seq, n_dp),
        out_shape=jax.ShapeDtypeStruct((features, tokens), bf16),
        in_specs=[pl.BlockSpec(memory_space=pltpu.SMEM)] * 2 + [pl.BlockSpec(memory_space=pl.ANY)] * 6,
        out_specs=pl.BlockSpec(memory_space=pltpu.VMEM),
        scratch_shapes=[
            wide, wide, pltpu.VMEM((heads, HS + 16, span), bf16), wide, wide,
            relay, relay, memories, memories,
            pltpu.VMEM((heads, span, 2 * HS), bf16),
            pltpu.VMEM((heads, HS + 16, mem_len), bf16),
            block, block, stats, block, stats,
            pltpu.VMEM((heads, HS, span), f32),
            pltpu.VMEM((1, span), f32),
            pltpu.VMEM((8, LANES), i32),
            pltpu.VMEM((n_dp, 8, LANES), i32),
            pltpu.VMEM((n_seg, 8, LANES), i32),
            dma((heads, 5)), dma((5,)), dma((2,)), dma((2,)), dma((2,)), dma((2,)), dma((heads,)), dma((heads,)),
            dma, dma, dma((n_dp,)), dma, pltpu.SemaphoreType.REGULAR, dma((n_seg,)), dma((n_seg,)), dma, dma,
        ],
        compiler_params=pltpu.CompilerParams(
            collective_id=0, has_side_effects=True, vmem_limit_bytes=56 * 2**20
        ),
    )(target, source, *flat, *memory)
    return out.reshape(1, 1, features, tokens)


def solution(mesh):
    sizes = [mesh.shape[name] for name in ("segment", "seq", "dp")]
    wide = P("segment", "dp", None, "seq")
    in_specs = (wide,) * 6 + (P("segment", "dp", None),) * 2
    return jax.shard_map(
        functools.partial(local, *sizes), mesh=mesh, in_specs=in_specs, out_specs=wide, check_vma=False
    )
```

```python
import functools

import jax
import jax.numpy as jnp
from jax import lax
from jax.experimental import pallas as pl
from jax.experimental.pallas import tpu as pltpu
from jax.sharding import PartitionSpec as P

HS = 64
SEQS = 2
BLOCK = 512
LANES = 128
MASKED = -1e30
MESH = pl.DeviceIdType.MESH
K, V, QU, Q, C = range(5)


def kernel(
    n_seg, n_seq, n_dp,
    target_hbm, source_hbm, dq_ref, dk_ref, dv_ref, cq_ref, mk_ref, mv_ref,
    out_ref,
    q_buf, k_buf, v_buf, c_buf, u_buf, rk_buf, rv_buf, mk_buf, mv_buf, kt_buf, mvt_buf,
    o_buf, part_buf, stat_buf, part_in, stat_in, acc_buf, weight_buf, len_own, len_dp, len_ring,
    in_sems, send_sems, relay_sems, relay_sends, mem_sems, mem_sends, part_sems, stat_sems,
    part_send, stat_send, dp_sems, dp_send, ready_sem, lower_sem, target_ref, source_ref, smem_sems, ring_sems, ring_sends, out_sem, out_send,
):
    group = n_seq // SEQS
    pair = group // 2
    tokens = dq_ref.shape[1]
    span = pair * tokens
    seq_len = group * tokens
    mem_tokens = mk_ref.shape[0]
    heads = q_buf.shape[0]
    owned = heads * HS
    blocks = span // BLOCK
    per = BLOCK // LANES

    seg, place, dp = lax.axis_index("segment"), lax.axis_index("seq"), lax.axis_index("dp")
    which = place // group
    rank = place % group
    first = which * group
    upper = rank // pair
    part = rank % pair
    base = first + upper * pair
    later = {"segment": (seg + 1) % n_seg}
    early = {"segment": (seg + n_seg - 1) % n_seg}

    barrier = pltpu.get_barrier_semaphore()

    @pl.loop(1, pair)
    def _(step):
        pl.semaphore_signal(
            barrier, 1, device_id={"seq": base + (part + step) % pair}, device_id_type=MESH
        )

    @pl.when(upper == 1)
    def _():
        @pl.loop(0, pair)
        def _(step):
            pl.semaphore_signal(barrier, 1, device_id={"seq": first + step}, device_id_type=MESH)

    order = (dp % 2) * (n_dp // 2) + dp // 2

    def dp_at(turn):
        return {"dp": (turn % 2) * (n_dp // 2) + turn // 2}

    for turn in range(1, n_dp):

        @pl.when(turn > order)
        def _():
            pl.semaphore_signal(barrier, 1, device_id=dp_at(turn), device_id_type=MESH)

    @pl.when(seg < n_seg - 1)
    def _():
        pl.semaphore_signal(barrier, 1, device_id=later, device_id_type=MESH)

    @pl.when(seg == 0)
    def _():
        pl.semaphore_signal(barrier, 1, device_id=early, device_id_type=MESH)


    lengths = [
        pltpu.make_async_copy(src, dst, smem_sems.at[pos])
        for pos, (src, dst) in enumerate(((target_hbm, target_ref), (source_hbm, source_ref)))
    ]
    for copy in lengths:
        copy.start()
    for copy in lengths:
        copy.wait()
    target = target_ref[0, 0, which]
    source = source_ref[0, 0, which]

    row = lax.broadcasted_iota(jnp.int32, (HS, span), 0)
    column = upper * span + lax.broadcasted_iota(jnp.int32, (HS, span), 1)
    one_row = jnp.where(row == 0, 1.0, 0.0).astype(jnp.bfloat16)
    mask_row = jnp.where((row == 0) & (column >= target), MASKED, 0.0).astype(jnp.bfloat16)
    for h in range(heads):
        q_buf[h, HS:, :] = one_row
        u_buf[h, HS:, :] = one_row
        k_buf[h, HS:, :] = mask_row
        v_buf[h, HS:, :] = one_row[:16]
        c_buf[h, (1 - h % 2) * HS : (2 - h % 2) * HS, :] = one_row
    lens = jnp.full(len_own.shape, target_ref[0, 0, 0] + target_ref[0, 0, 1], jnp.int32)
    len_own[...] = lens
    len_dp[order] = lens

    first_here = jnp.where(seg > 0, 1, 0) + jnp.where(seg == n_seg - 1, 1, 0)
    upper_here = pair * (1 - upper)
    pl.semaphore_wait(barrier, pair - 1 + upper_here + order + first_here)

    @pl.when(upper == 0)
    def _():
        @pl.loop(0, pair)
        def _(step):
            pl.semaphore_signal(lower_sem, 1, device_id={"seq": first + pair + step}, device_id_type=MESH)

    @pl.when(seg > 0)
    def _():
        pl.semaphore_signal(ready_sem, 1, device_id=early, device_id_type=MESH)

    def remote(src, dst, send, recv, device):
        pltpu.make_async_remote_copy(
            src_ref=src, dst_ref=dst, send_sem=send, recv_sem=recv, device_id=device, device_id_type=MESH
        ).start()

    def drain(ref, sem):
        pltpu.make_async_copy(ref, ref, sem).wait()

    def aligned(start, size):
        return pl.ds(pl.multiple_of(start, size), size)

    def send_lengths(turn):
        remote(len_own, len_dp.at[order], dp_send, dp_sems.at[order], dp_at(turn))

    def take_lengths(turn):
        drain(len_dp.at[turn], dp_sems.at[turn])

    for turn in range(n_dp - 1):

        @pl.when(turn < order)
        def _():
            send_lengths(turn)

    lanes_own = aligned(part * tokens, tokens)
    kinds = {K: (dk_ref, k_buf), V: (dv_ref, v_buf), QU: (dq_ref, u_buf), Q: (dq_ref, q_buf), C: (cq_ref, c_buf)}

    def send_head(h, which_kinds):
        for kind in which_kinds:
            src, buf = kinds[kind]
            shift = (h % 2) * HS if kind == C else 0
            dst = buf.at[h, pl.ds(shift, HS), lanes_own]
            sem = in_sems.at[h, kind]

            def rows(to):
                return src.at[pl.ds(pl.multiple_of(to * owned, owned) + h * HS, HS)]

            if kind == QU:

                @pl.when(upper == 1)
                def _():
                    @pl.loop(0, pair)
                    def _(step):
                        to = (part + step) % pair
                        remote(rows(to), dst, send_sems.at[kind], sem, {"seq": first + to})

                continue

            pltpu.make_async_copy(rows(part), dst, sem).start()

            @pl.loop(1, pair)
            def _(step):
                to = (part + step) % pair
                remote(rows(to), dst, send_sems.at[kind], sem, {"seq": base + to})

    first_kinds, last_kinds = (K, V, QU), (Q, C)
    send_head(0, (K, V))

    @pl.when(upper == 1)
    def _():
        pl.semaphore_wait(lower_sem, pair)

    send_head(0, (QU,))
    send_head(1, first_kinds)
    send_head(0, last_kinds)

    @pl.when(seg < n_seg - 1)
    def _():
        pl.semaphore_wait(ready_sem, 1)

    for pos, (src, dst) in enumerate(((mk_ref, rk_buf), (mv_ref, rv_buf))):
        remote(src, dst, relay_sends.at[pos], relay_sems.at[pos], later)
    send_head(2, first_kinds)
    send_head(1, last_kinds)
    for turn in range(1, n_dp):

        @pl.when(turn > order)
        def _():
            take_lengths(turn)
            send_lengths(turn)

    for turn in range(n_dp - 1):

        @pl.when(turn < order)
        def _():
            take_lengths(turn)

    len_ring[0] = jnp.sum(len_dp[...], axis=0)
    remote(len_ring.at[0], len_ring.at[1], ring_sends.at[0], ring_sems.at[0], later)

    def pass_lengths(hop):
        drain(len_ring.at[hop], ring_sems.at[hop - 1])
        if hop < n_seg - 1:
            remote(len_ring.at[hop], len_ring.at[hop + 1], ring_sends.at[hop], ring_sems.at[hop], later)

    drain(rk_buf, relay_sems.at[0])
    drain(rv_buf, relay_sems.at[1])
    mem_rows = aligned(rank * mem_tokens, mem_tokens)

    def spread(to, move):
        for pos, (src, dst) in enumerate(((rk_buf, mk_buf), (rv_buf, mv_buf))):
            for couple in range(heads // 2):
                start = pl.multiple_of((to % pair) * owned, owned) + couple * LANES
                move(src.at[:, pl.ds(start, LANES)], dst.at[couple, mem_rows], pos)

    spread(rank, lambda src, dst, pos: pltpu.make_async_copy(src, dst, mem_sems.at[pos]).start())

    @pl.loop(1, group)
    def _(step):
        to = (rank + step) % group
        spread(
            to,
            lambda src, dst, pos: remote(src, dst, mem_sends.at[pos], mem_sems.at[pos], {"seq": first + to}),
        )

    for h in range(3, heads):
        send_head(h, first_kinds)
        send_head(h - 1, last_kinds)
    send_head(heads - 1, last_kinds)
    pass_lengths(1)

    def attend(keys, queries, values, causal):
        scores = jnp.dot(keys, queries, preferred_element_type=jnp.float32)
        if causal:
            rows = scores.shape[0] - BLOCK
            i = lax.broadcasted_iota(jnp.int32, (BLOCK, BLOCK), 1)
            j = lax.broadcasted_iota(jnp.int32, (BLOCK, BLOCK), 0)
            last = jnp.where(j <= i, scores[rows:], MASKED)
            scores = jnp.concatenate([scores[:rows], last], axis=0) if rows else last
        highest = jnp.max(scores, axis=0, keepdims=True)
        weights = jnp.exp(scores - highest).astype(jnp.bfloat16)
        both = jnp.dot(values, weights, preferred_element_type=jnp.float32)
        return both[:HS], both[HS : HS + 1], highest

    def causal_block(h, b):
        upto = (b + 1) * BLOCK
        return attend(kt_buf[h, :upto], q_buf[h, :, b * BLOCK : upto], v_buf[h, :, :upto], True)

    mem_len = mk_buf.shape[1]
    lane = lax.broadcasted_iota(jnp.int32, (mem_len, LANES), 1)
    token = lax.broadcasted_iota(jnp.int32, (mem_len, LANES), 0)
    part_bytes = part_buf.at[0]

    def columns(b):
        return slice(b * BLOCK, (b + 1) * BLOCK)

    def finish(h, b, self_part, cross_part):
        mixed = (self_part + cross_part[:, columns(b)]) * weight_buf[:, columns(b)]
        o_buf[h, :, columns(b)] = mixed.astype(jnp.bfloat16)
        dst = out_ref.at[pl.ds(pl.multiple_of(part * owned + h * HS, HS), HS)]
        for to in range(b * per, (b + 1) * per):
            src = o_buf.at[h, :, pl.ds(to * tokens, tokens)]

            @pl.when(part != to)
            def _():
                remote(src, dst, out_send, out_sem, {"seq": base + to})

            @pl.when(part == to)
            def _():
                pltpu.make_async_copy(src, dst, out_sem).start()

    def cross(h):
        both, summed, _ = attend(memory_keys(h), c_buf[h], mvt_buf[h], False)
        return both / summed

    def memory_keys(h):
        side = h % 2
        inside = (lane >= side * HS) & (lane < (side + 1) * HS)
        mask = jnp.where((lane == (1 - side) * HS) & (token >= source), MASKED, 0.0)
        return jnp.where(inside, mk_buf[h // 2], mask.astype(jnp.bfloat16))

    def put_stat(h, b, highest, summed):
        for e in range(per):
            cols = slice(e * LANES, (e + 1) * LANES)
            stat_buf[h * blocks + b, e : e + 1, :] = highest[:, cols]
            stat_buf[h * blocks + b, per + e : per + e + 1, :] = summed[:, cols]

    def get_stat(ref, h, b):
        return [
            jnp.concatenate([ref[h * blocks + b, at + e : at + e + 1, :] for e in range(per)], axis=1)
            for at in (0, per)
        ]

    def merge_head(h):
        wait_input(h, C)
        cross_part = cross(h)
        for b in range(blocks):
            drain(part_bytes.at[:, pl.ds(0, BLOCK)], part_sems.at[h * blocks + b])
            drain(stat_buf.at[0], stat_sems.at[h * blocks + b])
            high_u, sum_u = get_stat(stat_buf, h, b)
            high_l, sum_l = get_stat(stat_in, h, b)
            highest = jnp.maximum(high_u, high_l)
            keep_u, keep_l = jnp.exp(high_u - highest), sum_l * jnp.exp(high_l - highest)
            total = sum_u * keep_u + keep_l
            other = part_in[h, :, columns(b)].astype(jnp.float32)
            merged = acc_buf[h, :, columns(b)] * (keep_u / total) + other * (keep_l / total)
            finish(h, b, merged, cross_part)

    def wait_input(h, kind):
        drain(part_bytes, in_sems.at[h, kind])

    def take_memory():
        for hop in range(2, n_seg):
            pass_lengths(hop)
        live = jnp.sum(len_ring[...], axis=0)[0:1]
        scale = jnp.float32(n_seg * n_dp * SEQS * seq_len) / live.astype(jnp.float32)
        position = upper * span + lax.broadcasted_iota(jnp.int32, (1, span), 1)
        weight_buf[...] = jnp.where(position < target, jnp.concatenate([scale] * (span // LANES), axis=1), 0.0)
        drain(mk_buf, mem_sems.at[0])
        drain(mv_buf, mem_sems.at[1])
        ones = jnp.where(lax.broadcasted_iota(jnp.int32, (16, mem_len), 0) == 0, 1.0, 0.0).astype(jnp.bfloat16)
        for couple in range(heads // 2):
            values_t = mv_buf[couple].T
            for side in range(2):
                mvt_buf[2 * couple + side] = jnp.concatenate([values_t[side * HS : (side + 1) * HS], ones], axis=0)

    def take_keys(h):
        wait_input(h, K)
        wait_input(h, V)
        for j in range(0, span, LANES):
            kt_buf[h, j : j + LANES, :] = k_buf[h, :, j : j + LANES].T

    @pl.when(upper == 0)
    def _():
        opposite = {"seq": place + pair}

        @pl.loop(0, heads + 1)
        def _(step):
            @pl.when(step < heads)
            def _():
                h = step
                take_keys(h)
                wait_input(h, QU)
                for b in range(blocks):
                    both, summed, highest = attend(kt_buf[h], u_buf[h, :, columns(b)], v_buf[h], False)
                    part_buf[h, :, columns(b)] = (both / summed).astype(jnp.bfloat16)
                    put_stat(h, b, highest, summed)
                    index = h * blocks + b
                    cols = pl.ds(b * BLOCK, BLOCK)
                    remote(
                        part_buf.at[h, :, cols], part_in.at[h, :, cols], part_send, part_sems.at[index], opposite
                    )
                    remote(stat_buf.at[index], stat_in.at[index], stat_send, stat_sems.at[index], opposite)

            @pl.when(step == 1)
            def _():
                take_memory()

            @pl.when(step > 0)
            def _():
                h = step - 1
                wait_input(h, Q)
                wait_input(h, C)
                cross_part = cross(h)
                for b in range(blocks):
                    both, summed, _ = causal_block(h, b)
                    finish(h, b, both / summed, cross_part)

    @pl.when(upper == 1)
    def _():
        @pl.loop(0, heads)
        def _(h):
            take_keys(h)
            wait_input(h, Q)
            for b in range(blocks):
                both, summed, highest = causal_block(h, b)
                acc_buf[h, :, columns(b)] = both
                put_stat(h, b, highest, summed)

            @pl.when(h == 1)
            def _():
                take_memory()

            @pl.when(h > 0)
            def _():
                merge_head(h - 1)

    @pl.when(upper == 1)
    def _():
        merge_head(heads - 1)
        drain(part_buf, send_sems.at[QU])

    @pl.when(upper == 0)
    def _():
        drain(part_buf, part_send)
        drain(stat_buf, stat_send)

    if n_dp > 1:
        drain(len_dp.at[pl.ds(1, n_dp - 1)], dp_send)
    for hop in range(n_seg - 1):
        drain(len_ring.at[hop], ring_sends.at[hop])
    drain(rk_buf, relay_sends.at[0])
    drain(rv_buf, relay_sends.at[1])
    for pos, buf in enumerate((mk_buf, mv_buf)):
        drain(buf.at[:, pl.ds(0, mem_len - mem_tokens)], mem_sends.at[pos])
    for kind in (K, V, Q, C):
        drain(part_buf.at[:, :, pl.ds(0, span - tokens)], send_sems.at[kind])
    drain(o_buf.at[:, :, pl.ds(0, span - tokens)], out_send)
    drain(out_ref, out_sem)


def local(n_seg, n_seq, n_dp, dq, dk, dv, cq, mk, mv, target, source):
    features, tokens = dq.shape[2:]
    group = n_seq // SEQS
    pair = group // 2
    span = pair * tokens
    owned = features // pair
    heads = owned // HS
    mem_tokens = mk.shape[3]
    mem_len = group * mem_tokens
    flat = [a.reshape(features, tokens) for a in (dq, dk, dv, cq)]
    memory = [a.reshape(features, mem_tokens).T for a in (mk, mv)]
    bf16, f32, i32 = jnp.bfloat16, jnp.float32, jnp.int32
    dma = pltpu.SemaphoreType.DMA
    wide = pltpu.VMEM((heads, 2 * HS, span), bf16)
    block = pltpu.VMEM((heads, HS, span), bf16)
    blocks = span // BLOCK
    stats = pltpu.VMEM((heads * blocks, 2 * BLOCK // LANES, LANES), f32)
    relay = pltpu.VMEM((mem_tokens, features), bf16)
    memories = pltpu.VMEM((heads // 2, mem_len, LANES), bf16)
    out = pl.pallas_call(
        functools.partial(kernel, n_seg, n_seq, n_dp),
        out_shape=jax.ShapeDtypeStruct((features, tokens), bf16),
        in_specs=[pl.BlockSpec(memory_space=pl.ANY)] * 8,
        out_specs=pl.BlockSpec(memory_space=pl.ANY),
        scratch_shapes=[
            wide, wide, pltpu.VMEM((heads, HS + 16, span), bf16), wide, wide,
            relay, relay, memories, memories,
            pltpu.VMEM((heads, span, 2 * HS), bf16),
            pltpu.VMEM((heads, HS + 16, mem_len), bf16),
            block, block, stats, block, stats,
            pltpu.VMEM((heads, HS, span), f32),
            pltpu.VMEM((1, span), f32),
            pltpu.VMEM((8, LANES), i32),
            pltpu.VMEM((n_dp, 8, LANES), i32),
            pltpu.VMEM((n_seg, 8, LANES), i32),
            dma((heads, 5)), dma((5,)), dma((2,)), dma((2,)), dma((2,)), dma((2,)), dma((heads * blocks,)), dma((heads * blocks,)),
            dma, dma, dma((n_dp,)), dma, pltpu.SemaphoreType.REGULAR, pltpu.SemaphoreType.REGULAR,
            pltpu.SMEM((1, 1, SEQS), i32), pltpu.SMEM((1, 1, SEQS), i32), dma((2,)),
            dma((n_seg,)), dma((n_seg,)), dma, dma,
        ],
        compiler_params=pltpu.CompilerParams(
            collective_id=0, has_side_effects=True, vmem_limit_bytes=56 * 2**20
        ),
    )(target, source, *flat, *memory)
    return out.reshape(1, 1, features, tokens)


def solution(mesh):
    sizes = [mesh.shape[name] for name in ("segment", "seq", "dp")]
    wide = P("segment", "dp", None, "seq")
    in_specs = (wide,) * 6 + (P("segment", "dp", None),) * 2
    return jax.shard_map(
        functools.partial(local, *sizes), mesh=mesh, in_specs=in_specs, out_specs=wide, check_vma=False
    )
```

```python
import functools

import jax
import jax.numpy as jnp
from jax import lax
from jax.experimental import pallas as pl
from jax.experimental.pallas import tpu as pltpu
from jax.sharding import PartitionSpec as P

HS = 64
SEQS = 2
BLOCK = 512
LANES = 128
MASKED = -1e30
MESH = pl.DeviceIdType.MESH
K, V, QU, Q, C = range(5)


def kernel(
    n_seg, n_seq, n_dp,
    target_hbm, source_hbm, dq_ref, dk_ref, dv_ref, cq_ref, mk_ref, mv_ref,
    out_ref,
    q_buf, k_buf, v_buf, c_buf, u_buf, rk_buf, rv_buf, mk_buf, mv_buf, kt_buf, mvt_buf,
    o_buf, part_buf, stat_buf, part_in, stat_in, acc_buf, weight_buf, len_own, len_dp, len_ring,
    in_sems, send_sems, relay_sems, relay_sends, mem_sems, mem_sends, part_sems, stat_sems,
    part_send, stat_send, dp_sems, dp_send, ready_sem, lower_sem, target_ref, source_ref, smem_sems, ring_sems, ring_sends, out_sem, out_send,
):
    group = n_seq // SEQS
    pair = group // 2
    tokens = dq_ref.shape[1]
    span = pair * tokens
    seq_len = group * tokens
    mem_tokens = mk_ref.shape[0]
    heads = q_buf.shape[0]
    owned = heads * HS
    blocks = span // BLOCK
    per = BLOCK // LANES

    seg, place, dp = lax.axis_index("segment"), lax.axis_index("seq"), lax.axis_index("dp")
    which = place // group
    rank = place % group
    first = which * group
    upper = rank // pair
    part = rank % pair
    base = first + upper * pair
    later = {"segment": (seg + 1) % n_seg}
    early = {"segment": (seg + n_seg - 1) % n_seg}

    barrier = pltpu.get_barrier_semaphore()

    @pl.loop(1, pair)
    def _(step):
        pl.semaphore_signal(
            barrier, 1, device_id={"seq": base + (part + step) % pair}, device_id_type=MESH
        )

    @pl.when(upper == 1)
    def _():
        @pl.loop(0, pair)
        def _(step):
            pl.semaphore_signal(barrier, 1, device_id={"seq": first + step}, device_id_type=MESH)

    order = (dp % 2) * (n_dp // 2) + dp // 2

    def dp_at(turn):
        return {"dp": (turn % 2) * (n_dp // 2) + turn // 2}

    for turn in range(1, n_dp):

        @pl.when(turn > order)
        def _():
            pl.semaphore_signal(barrier, 1, device_id=dp_at(turn), device_id_type=MESH)

    @pl.when(seg < n_seg - 1)
    def _():
        pl.semaphore_signal(barrier, 1, device_id=later, device_id_type=MESH)

    @pl.when(seg == 0)
    def _():
        pl.semaphore_signal(barrier, 1, device_id=early, device_id_type=MESH)


    lengths = [
        pltpu.make_async_copy(src, dst, smem_sems.at[pos])
        for pos, (src, dst) in enumerate(((target_hbm, target_ref), (source_hbm, source_ref)))
    ]
    for copy in lengths:
        copy.start()
    for copy in lengths:
        copy.wait()
    target = target_ref[0, 0, which]
    source = source_ref[0, 0, which]

    row = lax.broadcasted_iota(jnp.int32, (HS, span), 0)
    column = upper * span + lax.broadcasted_iota(jnp.int32, (HS, span), 1)
    one_row = jnp.where(row == 0, 1.0, 0.0).astype(jnp.bfloat16)
    mask_row = jnp.where((row == 0) & (column >= target), MASKED, 0.0).astype(jnp.bfloat16)
    for h in range(heads):
        q_buf[h, HS:, :] = one_row
        u_buf[h, HS:, :] = one_row
        k_buf[h, HS:, :] = mask_row
        v_buf[h, HS:, :] = one_row[:16]
        c_buf[h, (1 - h % 2) * HS : (2 - h % 2) * HS, :] = one_row
    lens = jnp.full(len_own.shape, target_ref[0, 0, 0] + target_ref[0, 0, 1], jnp.int32)
    len_own[...] = lens
    len_dp[order] = lens

    first_here = jnp.where(seg > 0, 1, 0) + jnp.where(seg == n_seg - 1, 1, 0)
    upper_here = pair * (1 - upper)
    pl.semaphore_wait(barrier, pair - 1 + upper_here + order + first_here)

    @pl.when(upper == 0)
    def _():
        @pl.loop(0, pair)
        def _(step):
            pl.semaphore_signal(lower_sem, 1, device_id={"seq": first + pair + step}, device_id_type=MESH)

    @pl.when(seg > 0)
    def _():
        pl.semaphore_signal(ready_sem, 1, device_id=early, device_id_type=MESH)

    def remote(src, dst, send, recv, device):
        pltpu.make_async_remote_copy(
            src_ref=src, dst_ref=dst, send_sem=send, recv_sem=recv, device_id=device, device_id_type=MESH
        ).start()

    def drain(ref, sem):
        pltpu.make_async_copy(ref, ref, sem).wait()

    def aligned(start, size):
        return pl.ds(pl.multiple_of(start, size), size)

    def send_lengths(turn):
        remote(len_own, len_dp.at[order], dp_send, dp_sems.at[order], dp_at(turn))

    def take_lengths(turn):
        drain(len_dp.at[turn], dp_sems.at[turn])

    for turn in range(n_dp - 1):

        @pl.when(turn < order)
        def _():
            send_lengths(turn)

    lanes_own = aligned(part * tokens, tokens)
    kinds = {K: (dk_ref, k_buf), V: (dv_ref, v_buf), QU: (dq_ref, u_buf), Q: (dq_ref, q_buf), C: (cq_ref, c_buf)}

    def send_head(h, which_kinds):
        for kind in which_kinds:
            src, buf = kinds[kind]
            shift = (h % 2) * HS if kind == C else 0
            dst = buf.at[h, pl.ds(shift, HS), lanes_own]
            sem = in_sems.at[h, kind]

            def rows(to):
                return src.at[pl.ds(pl.multiple_of(to * owned, owned) + h * HS, HS)]

            if kind == QU:

                @pl.when(upper == 1)
                def _():
                    @pl.loop(0, pair)
                    def _(step):
                        to = (part + step) % pair
                        remote(rows(to), dst, send_sems.at[kind], sem, {"seq": first + to})

                continue

            pltpu.make_async_copy(rows(part), dst, sem).start()

            @pl.loop(0, pair - 1)
            def _(step):
                to = (part + 1 + (step + pair // 2 - 1) % (pair - 1)) % pair
                remote(rows(to), dst, send_sems.at[kind], sem, {"seq": base + to})

    first_kinds, last_kinds = (K, V, QU), (Q, C)
    send_head(0, (K, V))

    @pl.when(upper == 1)
    def _():
        pl.semaphore_wait(lower_sem, pair)

    send_head(0, (QU,))
    send_head(1, first_kinds)
    send_head(0, last_kinds)

    @pl.when(seg < n_seg - 1)
    def _():
        pl.semaphore_wait(ready_sem, 1)

    for pos, (src, dst) in enumerate(((mk_ref, rk_buf), (mv_ref, rv_buf))):
        remote(src, dst, relay_sends.at[pos], relay_sems.at[pos], later)
    send_head(2, first_kinds)
    send_head(1, last_kinds)
    for turn in range(1, n_dp):

        @pl.when(turn > order)
        def _():
            take_lengths(turn)
            send_lengths(turn)

    for turn in range(n_dp - 1):

        @pl.when(turn < order)
        def _():
            take_lengths(turn)

    len_ring[0] = jnp.sum(len_dp[...], axis=0)
    remote(len_ring.at[0], len_ring.at[1], ring_sends.at[0], ring_sems.at[0], later)

    def pass_lengths(hop):
        drain(len_ring.at[hop], ring_sems.at[hop - 1])
        if hop < n_seg - 1:
            remote(len_ring.at[hop], len_ring.at[hop + 1], ring_sends.at[hop], ring_sems.at[hop], later)

    drain(rk_buf, relay_sems.at[0])
    drain(rv_buf, relay_sems.at[1])
    mem_rows = aligned(rank * mem_tokens, mem_tokens)

    def spread(to, move):
        for pos, (src, dst) in enumerate(((rk_buf, mk_buf), (rv_buf, mv_buf))):
            for couple in range(heads // 2):
                start = pl.multiple_of((to % pair) * owned, owned) + couple * LANES
                move(src.at[:, pl.ds(start, LANES)], dst.at[couple, mem_rows], pos)

    spread(rank, lambda src, dst, pos: pltpu.make_async_copy(src, dst, mem_sems.at[pos]).start())

    @pl.loop(1, group)
    def _(step):
        to = (rank + step) % group
        spread(
            to,
            lambda src, dst, pos: remote(src, dst, mem_sends.at[pos], mem_sems.at[pos], {"seq": first + to}),
        )

    for h in range(3, heads):
        send_head(h, first_kinds)
        send_head(h - 1, last_kinds)
    send_head(heads - 1, last_kinds)
    pass_lengths(1)

    def attend(keys, queries, values, causal):
        scores = jnp.dot(keys, queries, preferred_element_type=jnp.float32)
        if causal:
            rows = scores.shape[0] - BLOCK
            i = lax.broadcasted_iota(jnp.int32, (BLOCK, BLOCK), 1)
            j = lax.broadcasted_iota(jnp.int32, (BLOCK, BLOCK), 0)
            last = jnp.where(j <= i, scores[rows:], MASKED)
            scores = jnp.concatenate([scores[:rows], last], axis=0) if rows else last
        highest = jnp.max(scores, axis=0, keepdims=True)
        weights = jnp.exp(scores - highest).astype(jnp.bfloat16)
        both = jnp.dot(values, weights, preferred_element_type=jnp.float32)
        return both[:HS], both[HS : HS + 1], highest

    def causal_block(h, b):
        upto = (b + 1) * BLOCK
        return attend(kt_buf[h, :upto], q_buf[h, :, b * BLOCK : upto], v_buf[h, :, :upto], True)

    mem_len = mk_buf.shape[1]
    lane = lax.broadcasted_iota(jnp.int32, (mem_len, LANES), 1)
    token = lax.broadcasted_iota(jnp.int32, (mem_len, LANES), 0)
    part_bytes = part_buf.at[0]

    def columns(b):
        return slice(b * BLOCK, (b + 1) * BLOCK)

    def finish(h, b, self_part, cross_part):
        mixed = (self_part + cross_part[:, columns(b)]) * weight_buf[:, columns(b)]
        o_buf[h, :, columns(b)] = mixed.astype(jnp.bfloat16)
        dst = out_ref.at[pl.ds(pl.multiple_of(part * owned + h * HS, HS), HS)]
        for to in range(b * per, (b + 1) * per):
            src = o_buf.at[h, :, pl.ds(to * tokens, tokens)]

            @pl.when(part != to)
            def _():
                remote(src, dst, out_send, out_sem, {"seq": base + to})

            @pl.when(part == to)
            def _():
                pltpu.make_async_copy(src, dst, out_sem).start()

    def cross(h):
        both, summed, _ = attend(memory_keys(h), c_buf[h], mvt_buf[h], False)
        return both / summed

    def memory_keys(h):
        side = h % 2
        inside = (lane >= side * HS) & (lane < (side + 1) * HS)
        mask = jnp.where((lane == (1 - side) * HS) & (token >= source), MASKED, 0.0)
        return jnp.where(inside, mk_buf[h // 2], mask.astype(jnp.bfloat16))

    def put_stat(h, b, highest, summed):
        for e in range(per):
            cols = slice(e * LANES, (e + 1) * LANES)
            stat_buf[h * blocks + b, e : e + 1, :] = highest[:, cols]
            stat_buf[h * blocks + b, per + e : per + e + 1, :] = summed[:, cols]

    def get_stat(ref, h, b):
        return [
            jnp.concatenate([ref[h * blocks + b, at + e : at + e + 1, :] for e in range(per)], axis=1)
            for at in (0, per)
        ]

    def merge_head(h):
        wait_input(h, C)
        cross_part = cross(h)
        for b in range(blocks):
            drain(part_bytes.at[:, pl.ds(0, BLOCK)], part_sems.at[h * blocks + b])
            drain(stat_buf.at[0], stat_sems.at[h * blocks + b])
            high_u, sum_u = get_stat(stat_buf, h, b)
            high_l, sum_l = get_stat(stat_in, h, b)
            highest = jnp.maximum(high_u, high_l)
            keep_u, keep_l = jnp.exp(high_u - highest), sum_l * jnp.exp(high_l - highest)
            total = sum_u * keep_u + keep_l
            other = part_in[h, :, columns(b)].astype(jnp.float32)
            merged = acc_buf[h, :, columns(b)] * (keep_u / total) + other * (keep_l / total)
            finish(h, b, merged, cross_part)

    def wait_input(h, kind):
        drain(part_bytes, in_sems.at[h, kind])

    def take_memory():
        for hop in range(2, n_seg):
            pass_lengths(hop)
        live = jnp.sum(len_ring[...], axis=0)[0:1]
        scale = jnp.float32(n_seg * n_dp * SEQS * seq_len) / live.astype(jnp.float32)
        position = upper * span + lax.broadcasted_iota(jnp.int32, (1, span), 1)
        weight_buf[...] = jnp.where(position < target, jnp.concatenate([scale] * (span // LANES), axis=1), 0.0)
        drain(mk_buf, mem_sems.at[0])
        drain(mv_buf, mem_sems.at[1])
        ones = jnp.where(lax.broadcasted_iota(jnp.int32, (16, mem_len), 0) == 0, 1.0, 0.0).astype(jnp.bfloat16)
        for couple in range(heads // 2):
            values_t = mv_buf[couple].T
            for side in range(2):
                mvt_buf[2 * couple + side] = jnp.concatenate([values_t[side * HS : (side + 1) * HS], ones], axis=0)

    def take_keys(h):
        wait_input(h, K)
        wait_input(h, V)
        for j in range(0, span, LANES):
            kt_buf[h, j : j + LANES, :] = k_buf[h, :, j : j + LANES].T

    @pl.when(upper == 0)
    def _():
        opposite = {"seq": place + pair}

        @pl.loop(0, heads + 1)
        def _(step):
            @pl.when(step < heads)
            def _():
                h = step
                take_keys(h)
                wait_input(h, QU)
                for b in range(blocks):
                    both, summed, highest = attend(kt_buf[h], u_buf[h, :, columns(b)], v_buf[h], False)
                    part_buf[h, :, columns(b)] = (both / summed).astype(jnp.bfloat16)
                    put_stat(h, b, highest, summed)
                    index = h * blocks + b
                    cols = pl.ds(b * BLOCK, BLOCK)
                    remote(
                        part_buf.at[h, :, cols], part_in.at[h, :, cols], part_send, part_sems.at[index], opposite
                    )
                    remote(stat_buf.at[index], stat_in.at[index], stat_send, stat_sems.at[index], opposite)

            @pl.when(step == 1)
            def _():
                take_memory()

            @pl.when(step > 0)
            def _():
                h = step - 1
                wait_input(h, Q)
                wait_input(h, C)
                cross_part = cross(h)
                for b in range(blocks):
                    both, summed, _ = causal_block(h, b)
                    finish(h, b, both / summed, cross_part)

    @pl.when(upper == 1)
    def _():
        @pl.loop(0, heads)
        def _(h):
            take_keys(h)
            wait_input(h, Q)
            for b in range(blocks):
                both, summed, highest = causal_block(h, b)
                acc_buf[h, :, columns(b)] = both
                put_stat(h, b, highest, summed)

            @pl.when(h == 1)
            def _():
                take_memory()

            @pl.when(h > 0)
            def _():
                merge_head(h - 1)

    @pl.when(upper == 1)
    def _():
        merge_head(heads - 1)
        drain(part_buf, send_sems.at[QU])

    @pl.when(upper == 0)
    def _():
        drain(part_buf, part_send)
        drain(stat_buf, stat_send)

    if n_dp > 1:
        drain(len_dp.at[pl.ds(1, n_dp - 1)], dp_send)
    for hop in range(n_seg - 1):
        drain(len_ring.at[hop], ring_sends.at[hop])
    drain(rk_buf, relay_sends.at[0])
    drain(rv_buf, relay_sends.at[1])
    for pos, buf in enumerate((mk_buf, mv_buf)):
        drain(buf.at[:, pl.ds(0, mem_len - mem_tokens)], mem_sends.at[pos])
    for kind in (K, V, Q, C):
        drain(part_buf.at[:, :, pl.ds(0, span - tokens)], send_sems.at[kind])
    drain(o_buf.at[:, :, pl.ds(0, span - tokens)], out_send)
    drain(out_ref, out_sem)


def local(n_seg, n_seq, n_dp, dq, dk, dv, cq, mk, mv, target, source):
    features, tokens = dq.shape[2:]
    group = n_seq // SEQS
    pair = group // 2
    span = pair * tokens
    owned = features // pair
    heads = owned // HS
    mem_tokens = mk.shape[3]
    mem_len = group * mem_tokens
    flat = [a.reshape(features, tokens) for a in (dq, dk, dv, cq)]
    memory = [a.reshape(features, mem_tokens).T for a in (mk, mv)]
    bf16, f32, i32 = jnp.bfloat16, jnp.float32, jnp.int32
    dma = pltpu.SemaphoreType.DMA
    wide = pltpu.VMEM((heads, 2 * HS, span), bf16)
    block = pltpu.VMEM((heads, HS, span), bf16)
    blocks = span // BLOCK
    stats = pltpu.VMEM((heads * blocks, 2 * BLOCK // LANES, LANES), f32)
    relay = pltpu.VMEM((mem_tokens, features), bf16)
    memories = pltpu.VMEM((heads // 2, mem_len, LANES), bf16)
    out = pl.pallas_call(
        functools.partial(kernel, n_seg, n_seq, n_dp),
        out_shape=jax.ShapeDtypeStruct((features, tokens), bf16),
        in_specs=[pl.BlockSpec(memory_space=pl.ANY)] * 8,
        out_specs=pl.BlockSpec(memory_space=pl.ANY),
        scratch_shapes=[
            wide, wide, pltpu.VMEM((heads, HS + 16, span), bf16), wide, wide,
            relay, relay, memories, memories,
            pltpu.VMEM((heads, span, 2 * HS), bf16),
            pltpu.VMEM((heads, HS + 16, mem_len), bf16),
            block, block, stats, block, stats,
            pltpu.VMEM((heads, HS, span), f32),
            pltpu.VMEM((1, span), f32),
            pltpu.VMEM((8, LANES), i32),
            pltpu.VMEM((n_dp, 8, LANES), i32),
            pltpu.VMEM((n_seg, 8, LANES), i32),
            dma((heads, 5)), dma((5,)), dma((2,)), dma((2,)), dma((2,)), dma((2,)), dma((heads * blocks,)), dma((heads * blocks,)),
            dma, dma, dma((n_dp,)), dma, pltpu.SemaphoreType.REGULAR, pltpu.SemaphoreType.REGULAR,
            pltpu.SMEM((1, 1, SEQS), i32), pltpu.SMEM((1, 1, SEQS), i32), dma((2,)),
            dma((n_seg,)), dma((n_seg,)), dma, dma,
        ],
        compiler_params=pltpu.CompilerParams(
            collective_id=0, has_side_effects=True, vmem_limit_bytes=56 * 2**20
        ),
    )(target, source, *flat, *memory)
    return out.reshape(1, 1, features, tokens)


def solution(mesh):
    sizes = [mesh.shape[name] for name in ("segment", "seq", "dp")]
    wide = P("segment", "dp", None, "seq")
    in_specs = (wide,) * 6 + (P("segment", "dp", None),) * 2
    return jax.shard_map(
        functools.partial(local, *sizes), mesh=mesh, in_specs=in_specs, out_specs=wide, check_vma=False
    )
```

```python
import functools

import jax
import jax.numpy as jnp
from jax import lax
from jax.experimental import pallas as pl
from jax.experimental.pallas import tpu as pltpu
from jax.sharding import PartitionSpec as P

HS = 64
SEQS = 2
BLOCK = 512
LANES = 128
MASKED = -1e30
MESH = pl.DeviceIdType.MESH
K, V, QU, Q, C = range(5)


def kernel(
    n_seg, n_seq, n_dp,
    target_hbm, source_hbm, dq_ref, dk_ref, dv_ref, cq_ref, mk_ref, mv_ref,
    out_ref,
    q_buf, k_buf, v_buf, c_buf, u_buf, rk_buf, rv_buf, mk_buf, mv_buf, kt_buf, mvt_buf,
    o_buf, part_buf, stat_buf, part_in, stat_in, acc_buf, weight_buf, len_own, len_dp, len_ring,
    in_sems, send_sems, relay_sems, relay_sends, mem_sems, mem_sends, part_sems, stat_sems,
    part_send, stat_send, dp_sems, dp_send, ready_sem, lower_sem, target_ref, source_ref, smem_sems, ring_sems, ring_sends, out_sem, out_send,
):
    group = n_seq // SEQS
    pair = group // 2
    tokens = dq_ref.shape[1]
    span = pair * tokens
    seq_len = group * tokens
    mem_tokens = mk_ref.shape[0]
    heads = q_buf.shape[0]
    owned = heads * HS
    blocks = span // BLOCK
    per = BLOCK // LANES

    seg, place, dp = lax.axis_index("segment"), lax.axis_index("seq"), lax.axis_index("dp")
    which = place // group
    rank = place % group
    first = which * group
    upper = rank // pair
    part = rank % pair
    base = first + upper * pair
    later = {"segment": (seg + 1) % n_seg}
    early = {"segment": (seg + n_seg - 1) % n_seg}

    barrier = pltpu.get_barrier_semaphore()

    @pl.loop(1, pair)
    def _(step):
        pl.semaphore_signal(
            barrier, 1, device_id={"seq": base + (part + step) % pair}, device_id_type=MESH
        )

    @pl.when(upper == 1)
    def _():
        @pl.loop(0, pair)
        def _(step):
            pl.semaphore_signal(barrier, 1, device_id={"seq": first + step}, device_id_type=MESH)

    order = (dp % 2) * (n_dp // 2) + dp // 2

    def dp_at(turn):
        return {"dp": (turn % 2) * (n_dp // 2) + turn // 2}

    for turn in range(1, n_dp):

        @pl.when(turn > order)
        def _():
            pl.semaphore_signal(barrier, 1, device_id=dp_at(turn), device_id_type=MESH)

    @pl.when(seg < n_seg - 1)
    def _():
        pl.semaphore_signal(barrier, 1, device_id=later, device_id_type=MESH)

    @pl.when(seg == 0)
    def _():
        pl.semaphore_signal(barrier, 1, device_id=early, device_id_type=MESH)


    lengths = [
        pltpu.make_async_copy(src, dst, smem_sems.at[pos])
        for pos, (src, dst) in enumerate(((target_hbm, target_ref), (source_hbm, source_ref)))
    ]
    for copy in lengths:
        copy.start()
    for copy in lengths:
        copy.wait()
    target = target_ref[0, 0, which]
    source = source_ref[0, 0, which]

    row = lax.broadcasted_iota(jnp.int32, (HS, span), 0)
    column = upper * span + lax.broadcasted_iota(jnp.int32, (HS, span), 1)
    one_row = jnp.where(row == 0, 1.0, 0.0).astype(jnp.bfloat16)
    mask_row = jnp.where((row == 0) & (column >= target), MASKED, 0.0).astype(jnp.bfloat16)
    for h in range(heads):
        q_buf[h, HS:, :] = one_row
        u_buf[h, HS:, :] = one_row
        k_buf[h, HS:, :] = mask_row
        v_buf[h, HS:, :] = one_row[:16]
        c_buf[h, (1 - h % 2) * HS : (2 - h % 2) * HS, :] = one_row
    lens = jnp.full(len_own.shape, target_ref[0, 0, 0] + target_ref[0, 0, 1], jnp.int32)
    len_own[...] = lens
    len_dp[order] = lens

    first_here = jnp.where(seg > 0, 1, 0) + jnp.where(seg == n_seg - 1, 1, 0)
    upper_here = pair * (1 - upper)
    pl.semaphore_wait(barrier, pair - 1 + upper_here + order + first_here)

    @pl.when(upper == 0)
    def _():
        @pl.loop(0, pair)
        def _(step):
            pl.semaphore_signal(lower_sem, 1, device_id={"seq": first + pair + step}, device_id_type=MESH)

    @pl.when(seg > 0)
    def _():
        pl.semaphore_signal(ready_sem, 1, device_id=early, device_id_type=MESH)

    def remote(src, dst, send, recv, device):
        pltpu.make_async_remote_copy(
            src_ref=src, dst_ref=dst, send_sem=send, recv_sem=recv, device_id=device, device_id_type=MESH
        ).start()

    def drain(ref, sem):
        pltpu.make_async_copy(ref, ref, sem).wait()

    def aligned(start, size):
        return pl.ds(pl.multiple_of(start, size), size)

    def send_lengths(turn):
        remote(len_own, len_dp.at[order], dp_send, dp_sems.at[order], dp_at(turn))

    def take_lengths(turn):
        drain(len_dp.at[turn], dp_sems.at[turn])

    for turn in range(n_dp - 1):

        @pl.when(turn < order)
        def _():
            send_lengths(turn)

    lanes_own = aligned(part * tokens, tokens)
    kinds = {K: (dk_ref, k_buf), V: (dv_ref, v_buf), QU: (dq_ref, u_buf), Q: (dq_ref, q_buf), C: (cq_ref, c_buf)}

    def send_head(h, which_kinds):
        for kind in which_kinds:
            src, buf = kinds[kind]
            shift = (h % 2) * HS if kind == C else 0
            dst = buf.at[h, pl.ds(shift, HS), lanes_own]
            sem = in_sems.at[h, kind]

            def rows(to):
                return src.at[pl.ds(pl.multiple_of(to * owned, owned) + h * HS, HS)]

            if kind == QU:

                @pl.when(upper == 1)
                def _():
                    @pl.loop(0, pair)
                    def _(step):
                        to = (part + step) % pair
                        remote(rows(to), dst, send_sems.at[kind], sem, {"seq": first + to})

                continue

            pltpu.make_async_copy(rows(part), dst, sem).start()

            @pl.loop(0, pair - 1)
            def _(step):
                to = (part + 1 + (step + pair // 2 - 1) % (pair - 1)) % pair
                remote(rows(to), dst, send_sems.at[kind], sem, {"seq": base + to})

    first_kinds, last_kinds = (QU, K, V), (Q, C)
    send_head(0, (K, V))

    @pl.when(upper == 1)
    def _():
        pl.semaphore_wait(lower_sem, pair)

    send_head(0, (QU,))
    send_head(1, first_kinds)
    send_head(0, last_kinds)

    @pl.when(seg < n_seg - 1)
    def _():
        pl.semaphore_wait(ready_sem, 1)

    for pos, (src, dst) in enumerate(((mk_ref, rk_buf), (mv_ref, rv_buf))):
        remote(src, dst, relay_sends.at[pos], relay_sems.at[pos], later)
    send_head(2, first_kinds)
    send_head(1, last_kinds)
    for turn in range(1, n_dp):

        @pl.when(turn > order)
        def _():
            take_lengths(turn)
            send_lengths(turn)

    for turn in range(n_dp - 1):

        @pl.when(turn < order)
        def _():
            take_lengths(turn)

    len_ring[0] = jnp.sum(len_dp[...], axis=0)
    remote(len_ring.at[0], len_ring.at[1], ring_sends.at[0], ring_sems.at[0], later)

    def pass_lengths(hop):
        drain(len_ring.at[hop], ring_sems.at[hop - 1])
        if hop < n_seg - 1:
            remote(len_ring.at[hop], len_ring.at[hop + 1], ring_sends.at[hop], ring_sems.at[hop], later)

    drain(rk_buf, relay_sems.at[0])
    drain(rv_buf, relay_sems.at[1])
    mem_rows = aligned(rank * mem_tokens, mem_tokens)

    def spread(to, move):
        for pos, (src, dst) in enumerate(((rk_buf, mk_buf), (rv_buf, mv_buf))):
            for couple in range(heads // 2):
                start = pl.multiple_of((to % pair) * owned, owned) + couple * LANES
                move(src.at[:, pl.ds(start, LANES)], dst.at[couple, mem_rows], pos)

    spread(rank, lambda src, dst, pos: pltpu.make_async_copy(src, dst, mem_sems.at[pos]).start())

    @pl.loop(1, group)
    def _(step):
        to = (rank + step) % group
        spread(
            to,
            lambda src, dst, pos: remote(src, dst, mem_sends.at[pos], mem_sems.at[pos], {"seq": first + to}),
        )

    for h in range(3, heads):
        send_head(h, first_kinds)
        send_head(h - 1, last_kinds)
    send_head(heads - 1, last_kinds)
    pass_lengths(1)

    def attend(keys, queries, values, causal):
        scores = jnp.dot(keys, queries, preferred_element_type=jnp.float32)
        if causal:
            rows = scores.shape[0] - BLOCK
            i = lax.broadcasted_iota(jnp.int32, (BLOCK, BLOCK), 1)
            j = lax.broadcasted_iota(jnp.int32, (BLOCK, BLOCK), 0)
            last = jnp.where(j <= i, scores[rows:], MASKED)
            scores = jnp.concatenate([scores[:rows], last], axis=0) if rows else last
        highest = jnp.max(scores, axis=0, keepdims=True)
        weights = jnp.exp(scores - highest).astype(jnp.bfloat16)
        both = jnp.dot(values, weights, preferred_element_type=jnp.float32)
        return both[:HS], both[HS : HS + 1], highest

    def causal_block(h, b):
        upto = (b + 1) * BLOCK
        return attend(kt_buf[h, :upto], q_buf[h, :, b * BLOCK : upto], v_buf[h, :, :upto], True)

    mem_len = mk_buf.shape[1]
    lane = lax.broadcasted_iota(jnp.int32, (mem_len, LANES), 1)
    token = lax.broadcasted_iota(jnp.int32, (mem_len, LANES), 0)
    part_bytes = part_buf.at[0]

    def columns(b):
        return slice(b * BLOCK, (b + 1) * BLOCK)

    def finish(h, b, self_part, cross_part):
        mixed = (self_part + cross_part[:, columns(b)]) * weight_buf[:, columns(b)]
        o_buf[h, :, columns(b)] = mixed.astype(jnp.bfloat16)
        dst = out_ref.at[pl.ds(pl.multiple_of(part * owned + h * HS, HS), HS)]
        for to in range(b * per, (b + 1) * per):
            src = o_buf.at[h, :, pl.ds(to * tokens, tokens)]

            @pl.when(part != to)
            def _():
                remote(src, dst, out_send, out_sem, {"seq": base + to})

            @pl.when(part == to)
            def _():
                pltpu.make_async_copy(src, dst, out_sem).start()

    def cross(h):
        both, summed, _ = attend(memory_keys(h), c_buf[h], mvt_buf[h], False)
        return both / summed

    def memory_keys(h):
        side = h % 2
        inside = (lane >= side * HS) & (lane < (side + 1) * HS)
        mask = jnp.where((lane == (1 - side) * HS) & (token >= source), MASKED, 0.0)
        return jnp.where(inside, mk_buf[h // 2], mask.astype(jnp.bfloat16))

    def put_stat(h, b, highest, summed):
        for e in range(per):
            cols = slice(e * LANES, (e + 1) * LANES)
            stat_buf[h * blocks + b, e : e + 1, :] = highest[:, cols]
            stat_buf[h * blocks + b, per + e : per + e + 1, :] = summed[:, cols]

    def get_stat(ref, h, b):
        return [
            jnp.concatenate([ref[h * blocks + b, at + e : at + e + 1, :] for e in range(per)], axis=1)
            for at in (0, per)
        ]

    def merge_head(h):
        wait_input(h, C)
        cross_part = cross(h)
        for b in range(blocks):
            drain(part_bytes.at[:, pl.ds(0, BLOCK)], part_sems.at[h * blocks + b])
            drain(stat_buf.at[0], stat_sems.at[h * blocks + b])
            high_u, sum_u = get_stat(stat_buf, h, b)
            high_l, sum_l = get_stat(stat_in, h, b)
            highest = jnp.maximum(high_u, high_l)
            keep_u, keep_l = jnp.exp(high_u - highest), sum_l * jnp.exp(high_l - highest)
            total = sum_u * keep_u + keep_l
            other = part_in[h, :, columns(b)].astype(jnp.float32)
            merged = acc_buf[h, :, columns(b)] * (keep_u / total) + other * (keep_l / total)
            finish(h, b, merged, cross_part)

    def wait_input(h, kind):
        drain(part_bytes, in_sems.at[h, kind])

    def take_memory():
        for hop in range(2, n_seg):
            pass_lengths(hop)
        live = jnp.sum(len_ring[...], axis=0)[0:1]
        scale = jnp.float32(n_seg * n_dp * SEQS * seq_len) / live.astype(jnp.float32)
        position = upper * span + lax.broadcasted_iota(jnp.int32, (1, span), 1)
        weight_buf[...] = jnp.where(position < target, jnp.concatenate([scale] * (span // LANES), axis=1), 0.0)
        drain(mk_buf, mem_sems.at[0])
        drain(mv_buf, mem_sems.at[1])
        ones = jnp.where(lax.broadcasted_iota(jnp.int32, (16, mem_len), 0) == 0, 1.0, 0.0).astype(jnp.bfloat16)
        for couple in range(heads // 2):
            values_t = mv_buf[couple].T
            for side in range(2):
                mvt_buf[2 * couple + side] = jnp.concatenate([values_t[side * HS : (side + 1) * HS], ones], axis=0)

    def take_keys(h):
        wait_input(h, K)
        wait_input(h, V)
        for j in range(0, span, LANES):
            kt_buf[h, j : j + LANES, :] = k_buf[h, :, j : j + LANES].T

    @pl.when(upper == 0)
    def _():
        opposite = {"seq": place + pair}

        @pl.loop(0, heads + 1)
        def _(step):
            @pl.when(step < heads)
            def _():
                h = step
                take_keys(h)
                wait_input(h, QU)
                for b in range(blocks):
                    both, summed, highest = attend(kt_buf[h], u_buf[h, :, columns(b)], v_buf[h], False)
                    part_buf[h, :, columns(b)] = (both / summed).astype(jnp.bfloat16)
                    put_stat(h, b, highest, summed)
                    index = h * blocks + b
                    cols = pl.ds(b * BLOCK, BLOCK)
                    remote(
                        part_buf.at[h, :, cols], part_in.at[h, :, cols], part_send, part_sems.at[index], opposite
                    )
                    remote(stat_buf.at[index], stat_in.at[index], stat_send, stat_sems.at[index], opposite)

            @pl.when(step == 1)
            def _():
                take_memory()

            @pl.when(step > 0)
            def _():
                h = step - 1
                wait_input(h, Q)
                wait_input(h, C)
                cross_part = cross(h)
                for b in range(blocks):
                    both, summed, _ = causal_block(h, b)
                    finish(h, b, both / summed, cross_part)

    @pl.when(upper == 1)
    def _():
        @pl.loop(0, heads)
        def _(h):
            take_keys(h)
            wait_input(h, Q)
            for b in range(blocks):
                both, summed, highest = causal_block(h, b)
                acc_buf[h, :, columns(b)] = both
                put_stat(h, b, highest, summed)

            @pl.when(h == 1)
            def _():
                take_memory()

            @pl.when(h > 0)
            def _():
                merge_head(h - 1)

    @pl.when(upper == 1)
    def _():
        merge_head(heads - 1)
        drain(part_buf, send_sems.at[QU])

    @pl.when(upper == 0)
    def _():
        drain(part_buf, part_send)
        drain(stat_buf, stat_send)

    if n_dp > 1:
        drain(len_dp.at[pl.ds(1, n_dp - 1)], dp_send)
    for hop in range(n_seg - 1):
        drain(len_ring.at[hop], ring_sends.at[hop])
    drain(rk_buf, relay_sends.at[0])
    drain(rv_buf, relay_sends.at[1])
    for pos, buf in enumerate((mk_buf, mv_buf)):
        drain(buf.at[:, pl.ds(0, mem_len - mem_tokens)], mem_sends.at[pos])
    for kind in (K, V, Q, C):
        drain(part_buf.at[:, :, pl.ds(0, span - tokens)], send_sems.at[kind])
    drain(o_buf.at[:, :, pl.ds(0, span - tokens)], out_send)
    drain(out_ref, out_sem)


def local(n_seg, n_seq, n_dp, dq, dk, dv, cq, mk, mv, target, source):
    features, tokens = dq.shape[2:]
    group = n_seq // SEQS
    pair = group // 2
    span = pair * tokens
    owned = features // pair
    heads = owned // HS
    mem_tokens = mk.shape[3]
    mem_len = group * mem_tokens
    flat = [a.reshape(features, tokens) for a in (dq, dk, dv, cq)]
    memory = [a.reshape(features, mem_tokens).T for a in (mk, mv)]
    bf16, f32, i32 = jnp.bfloat16, jnp.float32, jnp.int32
    dma = pltpu.SemaphoreType.DMA
    wide = pltpu.VMEM((heads, 2 * HS, span), bf16)
    block = pltpu.VMEM((heads, HS, span), bf16)
    blocks = span // BLOCK
    stats = pltpu.VMEM((heads * blocks, 2 * BLOCK // LANES, LANES), f32)
    relay = pltpu.VMEM((mem_tokens, features), bf16)
    memories = pltpu.VMEM((heads // 2, mem_len, LANES), bf16)
    out = pl.pallas_call(
        functools.partial(kernel, n_seg, n_seq, n_dp),
        out_shape=jax.ShapeDtypeStruct((features, tokens), bf16),
        in_specs=[pl.BlockSpec(memory_space=pl.ANY)] * 8,
        out_specs=pl.BlockSpec(memory_space=pl.ANY),
        scratch_shapes=[
            wide, wide, pltpu.VMEM((heads, HS + 16, span), bf16), wide, wide,
            relay, relay, memories, memories,
            pltpu.VMEM((heads, span, 2 * HS), bf16),
            pltpu.VMEM((heads, HS + 16, mem_len), bf16),
            block, block, stats, block, stats,
            pltpu.VMEM((heads, HS, span), f32),
            pltpu.VMEM((1, span), f32),
            pltpu.VMEM((8, LANES), i32),
            pltpu.VMEM((n_dp, 8, LANES), i32),
            pltpu.VMEM((n_seg, 8, LANES), i32),
            dma((heads, 5)), dma((5,)), dma((2,)), dma((2,)), dma((2,)), dma((2,)), dma((heads * blocks,)), dma((heads * blocks,)),
            dma, dma, dma((n_dp,)), dma, pltpu.SemaphoreType.REGULAR, pltpu.SemaphoreType.REGULAR,
            pltpu.SMEM((1, 1, SEQS), i32), pltpu.SMEM((1, 1, SEQS), i32), dma((2,)),
            dma((n_seg,)), dma((n_seg,)), dma, dma,
        ],
        compiler_params=pltpu.CompilerParams(
            collective_id=0, has_side_effects=True, vmem_limit_bytes=56 * 2**20
        ),
    )(target, source, *flat, *memory)
    return out.reshape(1, 1, features, tokens)


def solution(mesh):
    sizes = [mesh.shape[name] for name in ("segment", "seq", "dp")]
    wide = P("segment", "dp", None, "seq")
    in_specs = (wide,) * 6 + (P("segment", "dp", None),) * 2
    return jax.shard_map(
        functools.partial(local, *sizes), mesh=mesh, in_specs=in_specs, out_specs=wide, check_vma=False
    )
```
